32 devices in a mesh: replica: 2 (over x), shard: 16 (over z, y, core).
Axes of the slice: x: 2, y: 2, z: 4, core: 2. Of those that a mesh axis runs over, the one named last changes fastest.
Arguments:
- tokens: bfloat16 [8192, 2048], P(('replica', 'shard')), may hold values from -6 to 6
- segments: int32 [32, 256], P(('replica', 'shard')), may hold values from 0 to 3, never falling along the last dimension, each value on 1 to 128 neighbouring positions
- attend_weight: bfloat16 [2048, 6144], P('shard'), may hold values from -0.125 to 0.125
- attend_bias: bfloat16 [6144], P('shard'), may hold values from -3 to 3
- output_weight: bfloat16 [2048, 2048], P('shard'), may hold values from -0.75 to 0.75
- attend_gain: bfloat16 [2048], P('shard'), may hold values from 0.5 to 1.5
- attend_shift: bfloat16 [2048], P('shard'), may hold values from -1 to 1
- expand_weight: bfloat16 [2048, 11264], P('shard'), may hold values from -0.125 to 0.125
- shrink_weight: bfloat16 [2048, 5632], P('shard'), may hold values from -0.15625 to 0.15625
- dense_gain: bfloat16 [2048], P('shard'), may hold values from 0.5 to 1.5
- dense_shift: bfloat16 [2048], P('shard'), may hold values from -1 to 1
- cotangent: bfloat16 [8192, 2048], P(('replica', 'shard')), may hold values from -6 to 6
Outputs:
- layer_output: bfloat16 [8192, 2048], P(('replica', 'shard'))
- tokens_gradient: bfloat16 [8192, 2048], P(('replica', 'shard'))
- attend_weight_gradient: float32 [2048, 6144], P('shard')
- attend_bias_gradient: float32 [6144], P('shard')
- output_weight_gradient: float32 [2048, 2048], P('shard')
- attend_gain_gradient: float32 [2048], P('shard')
- attend_shift_gradient: float32 [2048], P('shard')
- expand_weight_gradient: float32 [2048, 11264], P('shard')
- shrink_weight_gradient: float32 [2048, 5632], P('shard')
- dense_gain_gradient: float32 [2048], P('shard')
- dense_shift_gradient: float32 [2048], P('shard')
The draws below stay inside these ranges and needn't reach their ends.
Inputs may be any that keep to these rules, and one draw needn't show every extreme that they name: `segments`: along each sequence the segment numbers never fall, and a segment holds at most 128 tokens.
All inputs are finite; a program needn't handle non-finite values.
Results may differ from the reference program's by a relative error of at most 0.015.
Values may be sent and summed in bfloat16 or wider, within the bound.
No kernel may reach another device: no remote copies, remote signals or barrier semaphores. Data moves between devices by JAX's collectives and lax.ppermute only.
A program may use at most 640 MiB of HBM per device.

```python
import math
import jax
import jax.numpy as jnp
import numpy as np
from jax import lax

D = 2048
HEADS = 32
HEAD_DIM = 64
FF = 5632
ROT = 16
TOK_DEV = 256
SEQS = 32
TOKENS = 8192


def with_spikes(values, rng, source, target, shards_of, factor):
    owner, partner = [(jnp.arange(values.shape[dim]) // (values.shape[dim] // shards_of)).reshape([-1 if axis == dim else 1 for axis in range(values.ndim)]) for dim in (source, target)]
    chosen = jax.random.permutation(rng, shards_of)[partner]
    strong = (owner == chosen) | (owner == (partner + shards_of // 2) % shards_of)
    return jnp.where(strong, factor * values, values)


def level_of(own_key, dims, shards, smallest, top_value):
    def one(dim, blocks):
        heights = jax.random.uniform(jax.random.fold_in(jax.random.fold_in(own_key, 6), dim), (blocks,), jnp.float32, smallest / len(shards), top_value / len(shards))
        return jnp.repeat(jnp.exp(heights), dims[dim] // blocks).reshape((-1,) + (1,) * (len(dims) - dim - 1))

    loudness = one(*shards[0])
    for cut in shards[1:]:
        loudness = loudness * one(*cut)
    return loudness


def split_up(number_of, total, reach, skew):
    portions = [(1 << 20) // math.isqrt(rank ** skew) + 1 for rank in range(2, number_of + 1)]
    surplus, holding = total - reach - (number_of - 1), [1] * (number_of - 1)
    while surplus > 0:
        free = [i for i in range(number_of - 1) if holding[i] < reach]
        whole, budget = sum([portions[i] for i in free]), surplus
        for i in free:
            extra = min(reach - holding[i], max(1, budget * portions[i] // whole), surplus)
            holding[i] = holding[i] + extra
            surplus = surplus - extra
    return np.array([reach] + holding)


def uneven(own_key, amount, total, most, slope):
    if amount == 2:
        one = jax.random.randint(own_key, (), max(1, total - most), min(most, total - 1) + 1)
        return jnp.stack([one, total - one])
    lengths = jnp.asarray(split_up(amount, total, most, slope), jnp.int32)
    pairs = (amount - 1) // 2
    giver, sink = lengths[1:1 + 2 * pairs:2], lengths[2:2 + 2 * pairs:2]
    slack = jnp.minimum(giver - 1, most - sink)
    shifted = jax.random.randint(jax.random.fold_in(own_key, 1), (pairs,), 0, 1 << 20) % (slack + 1)
    lengths = lengths.at[1:1 + 2 * pairs:2].set(giver - shifted).at[2:2 + 2 * pairs:2].set(sink + shifted)
    return lengths[jax.random.permutation(jax.random.fold_in(own_key, 2), amount)]


def scatter_about(key, extent, width, bound, pieces=(), held_as=jnp.bfloat16):
    values = width * jax.random.normal(key, extent, jnp.float32)
    if pieces:
        values = values * level_of(key, extent, pieces, -0.22, 0.18)
    return jnp.clip(values, -bound, bound).astype(held_as)


def noise_with(own_key, extent, spread, reach, split, heavy, held_as=jnp.bfloat16):
    entries = spread * jax.random.normal(own_key, extent, jnp.float32)
    if split:
        entries = entries * level_of(own_key, extent, split, -0.22, 0.18)
    return jnp.clip(with_spikes(entries, jax.random.fold_in(own_key, 3), *heavy), -reach, reach).astype(held_as)


def setup_inputs(seed: int = 0) -> dict:
    splits = jax.random.split(jax.random.key(seed), 13)
    return {
        "tokens": noise_with(splits[0], (TOKENS, D), 1.0, 6.0, ((0, 32),), (0, 1, 32, 2.75)),
        "segments": jax.vmap(lambda own: jnp.searchsorted(jnp.cumsum(uneven(own, 4, TOK_DEV, TOK_DEV // 2, 1)), jnp.arange(TOK_DEV), side="right"))(jax.random.split(splits[1], SEQS)).reshape((SEQS, TOK_DEV)).astype(jnp.int32),
        "attend_weight": scatter_about(splits[2], (D, 3 * D), D ** -0.5, 0.125, ((0, 16),)),
        "attend_bias": scatter_about(splits[3], (3 * D,), 0.5, 3.0, ((0, 16),)),
        "output_weight": scatter_about(splits[4], (D, D), (D // 32) ** -0.5, 0.75, ((0, 16),)),
        "attend_gain": jnp.clip(1.0 + 0.1 * jax.random.normal(splits[5], (D,), jnp.float32), 0.5, 1.5).astype(jnp.bfloat16),
        "attend_shift": scatter_about(splits[6], (D,), 0.2, 1.0, ((0, 16),)),
        "expand_weight": scatter_about(splits[7], (D, 2 * FF), D ** -0.5, 0.125, ((0, 16),)),
        "shrink_weight": scatter_about(splits[8], (D, FF), (FF // 4) ** -0.5, 0.15625, ((0, 16),)),
        "dense_gain": jnp.clip(1.0 + 0.1 * jax.random.normal(splits[9], (D,), jnp.float32), 0.5, 1.5).astype(jnp.bfloat16),
        "dense_shift": scatter_about(splits[10], (D,), 0.2, 1.0, ((0, 16),)),
        "cotangent": noise_with(splits[11], (TOKENS, D), 1.0, 6.0, ((0, 32),), (0, 1, 32, 2.75)),
    }


@jax.custom_vjp
def low(v):
    return lax.optimization_barrier(v.astype(jnp.bfloat16)).astype(jnp.float32)

@jax.custom_vjp
def low_back(v):
    return v

def low_keep(v):
    return (low(v), None)

def low_pass(kept, grad):
    return (grad,)

def back_keep(v):
    return (v, None)

def back_low(kept, grad):
    return (low(grad),)
low.defvjp(low_keep, low_pass)
low_back.defvjp(back_keep, back_low)
EPSILON = 1e-05
HIGHEST = lax.Precision.HIGHEST

def layer_norm(values, gain_row, shift_row):
    center = lax.optimization_barrier(jnp.mean(values, axis=-1, keepdims=True))
    centered = values - center
    variance = lax.optimization_barrier(jnp.mean(centered * centered, axis=-1, keepdims=True))
    return centered * lax.rsqrt(variance + EPSILON) * gain_row + shift_row

def matmul(left_side, right_side):
    return jnp.dot(left_side, right_side, precision=HIGHEST, preferred_element_type=jnp.float32)

def rotary_tables(segment_row):
    length = segment_row.shape[0]
    places = jnp.arange(length)
    same_doc = segment_row[:, None] == segment_row[None, :]
    earlier = places[:, None] > places[None, :]
    position = lax.optimization_barrier(jnp.sum(jnp.where(same_doc & earlier, 1.0, 0.0), axis=1)).astype(jnp.float32)
    frequency = jnp.exp(jnp.arange(ROT // 2).astype(jnp.float32) * (-2.0 * math.log(10000.0) / ROT))
    angles = position[:, None] * frequency[None, :]
    allowed = same_doc & (places[:, None] >= places[None, :])
    return (jnp.cos(angles), jnp.sin(angles), allowed)

def rotate(values, cosines, sine_table):
    half_rot = ROT // 2
    first_half = values[..., :half_rot]
    second_half = values[..., half_rot:ROT]
    cos_wide = cosines[:, None, :]
    sin_wide = sine_table[:, None, :]
    return jnp.concatenate([first_half * cos_wide - second_half * sin_wide, second_half * cos_wide + first_half * sin_wide, values[..., ROT:]], axis=-1)

def attend(packed):
    joined, segment_row = packed
    length = joined.shape[0]
    cosines, sine_table, allowed = rotary_tables(segment_row)
    shaped = joined.reshape(length, 3, HEADS, HEAD_DIM)
    queries = low(rotate(shaped[:, 0], cosines, sine_table))
    keys_all = low(rotate(shaped[:, 1], cosines, sine_table))
    values_all = low(shaped[:, 2])
    scores = low_back(jnp.einsum('thd,shd->hts', queries, keys_all, precision=HIGHEST) * HEAD_DIM ** (-0.5))
    scores = jnp.where(allowed[None], scores, -1e+30)
    weights = low(jax.nn.softmax(scores, axis=-1))
    attended = jnp.einsum('hts,shd->thd', weights, values_all, precision=HIGHEST)
    return low(low_back(attended.reshape(length, D)))

def forward(params, token_rows, segment_rows):
    attend_weight, attend_bias, output_weight, attend_gain, attend_shift, expand_weight, shrink_weight, dense_gain, dense_shift = params
    groups, length, features = token_rows.shape
    flattened = token_rows.reshape(groups * length, features)
    attend_input = low(layer_norm(flattened, attend_gain, attend_shift))
    joined = low_back(matmul(attend_input, attend_weight) + attend_bias)
    attended = lax.map(jax.checkpoint(attend), (joined.reshape(groups, length, 3 * D), segment_rows))
    branch = low_back(matmul(attended.reshape(groups * length, D), output_weight.T))
    middle = flattened + branch
    dense_input = low(layer_norm(middle, dense_gain, dense_shift))
    gate_up = low_back(matmul(dense_input, expand_weight))
    hidden = low(jax.nn.silu(gate_up[:, :FF]) * gate_up[:, FF:])
    result = middle + low_back(matmul(hidden, shrink_weight.T))
    return result.reshape(groups, length, features)

def add_pair(running, update):
    return running + update

def reference(tokens, segments, attend_weight, attend_bias, output_weight, attend_gain, attend_shift, expand_weight, shrink_weight, dense_gain, dense_shift, cotangent):
    params = tuple((member.astype(jnp.float32) for member in (attend_weight, attend_bias, output_weight, attend_gain, attend_shift, expand_weight, shrink_weight, dense_gain, dense_shift)))
    per_step = math.gcd(SEQS, max(1, 4096 // TOK_DEV))
    sections = SEQS // per_step
    token_rows = tokens.astype(jnp.float32).reshape(sections, per_step, TOK_DEV, D)
    segment_rows = segments.reshape(sections, per_step, TOK_DEV)
    cotangent_rows = cotangent.astype(jnp.float32).reshape(sections, per_step, TOK_DEV, D)

    def one_section(running, packed):
        rows_now, segments_now, cotangent_now = packed

        def apply_layer(layer_params, layer_rows):
            return forward(layer_params, layer_rows, segments_now)
        result, pullback = jax.vjp(apply_layer, params, rows_now)
        param_slopes, row_slopes = pullback(cotangent_now)
        running = jax.tree.map(add_pair, running, param_slopes)
        return (running, (result.astype(jnp.bfloat16), row_slopes.astype(jnp.bfloat16)))
    initial = tuple((jnp.zeros(member.shape, jnp.float32) for member in params))
    totals, (results, slopes) = lax.scan(one_section, initial, (token_rows, segment_rows, cotangent_rows))
    return (results.reshape(TOKENS, D), slopes.reshape(TOKENS, D), totals[0], totals[1], totals[2], totals[3], totals[4], totals[5], totals[6], totals[7], totals[8])
```

```python
import math

import jax
import jax.numpy as jnp
from jax import lax
from jax.experimental import pallas as pl
from jax.experimental.pallas import tpu as pltpu
from jax.sharding import Mesh
from jax.sharding import PartitionSpec as P

D = 2048
HEADS = 32
HEAD_DIM = 64
FF = 5632
ROT = 16
PARTS = 4
PART_HEADS = HEADS // PARTS
PART_D = D // PARTS
PART_FF = FF // PARTS

EPSILON = 1e-05
F32 = jnp.float32
BF16 = jnp.bfloat16
SWAP = [(0, 1), (1, 0)]
CORE_PIECES = 2
NO_COST = pl.CostEstimate(flops=0, bytes_accessed=0, transcendentals=0)


def over_x(value):
    return lax.ppermute(value, "x", SWAP)


def over_y(value):
    return lax.ppermute(value, "y", SWAP)


def near_start(block):
    half = block.shape[0] // 2
    return over_x(block[:half]), over_y(block[half:])


def near_end(block, arrived):
    half = block.shape[0] // 2
    return jnp.concatenate([block[:half], arrived[0]]), jnp.concatenate([block[half:], arrived[1]])


def gather_far(near):
    return over_y(near[0]), over_x(near[1])


def gather_tokens(block):
    near = near_end(block, near_start(block))
    return jnp.concatenate([*near, *gather_far(near)])


def scatter_first(far):
    half = far.shape[0] // 4
    return over_y(far[: 2 * half]), over_x(far[2 * half :])


def scatter_second(near, sent):
    half = near.shape[0] // 4
    low = near[: 2 * half] + sent[0].astype(F32)
    high = near[2 * half :] + sent[1].astype(F32)
    last = over_x(low[half:].astype(BF16)), over_y(high[half:].astype(BF16))
    return low[:half], high[:half], *last


def scatter_end(low, high, low_last, high_last):
    return jnp.concatenate([low + low_last.astype(F32), high + high_last.astype(F32)])


def scatter_product(left_side, right_side, product):
    count = left_side.shape[0] // 2
    far = product(left_side[count:], right_side)
    sent = scatter_first(far)
    near = product(after(left_side, far)[:count], right_side)
    return scatter_end(*scatter_second(near, after(sent, near)))


def transposed(flip):
    return [(y * 2 + c, (1 - c if flip else c) * 2 + y) for y in range(2) for c in range(2)]


def turned_back(flip):
    return [(target, source) for source, target in transposed(flip)]


def columns(weight, groups, part):
    width = weight.shape[1] // (groups * PARTS)
    return jnp.concatenate(
        [
            lax.dynamic_slice_in_dim(weight, (g * PARTS + part) * width, width, axis=1)
            for g in range(groups)
        ],
        axis=1,
    )


def turn_start(*weights_and_groups):
    x, c = lax.axis_index("x"), lax.axis_index("c")

    def part_of(part):
        return jnp.concatenate([columns(w, g, part) for w, g in weights_and_groups], axis=1)

    first = lax.ppermute(part_of(2 * x + c), ("y", "c"), transposed(False))
    second = lax.ppermute(part_of(2 * x + 1 - c), ("y", "c"), transposed(True))
    return first, second


def turn_end(first, second):
    straight = lax.axis_index("y") == 0
    return jnp.concatenate(
        [jnp.where(straight, first, second), jnp.where(straight, second, first)]
    )


def gather_pair(pair):
    return lax.all_gather(pair, ("z", "c"), axis=0, tiled=True)


def scatter_pair(partial):
    return lax.psum_scatter(partial, "z", scatter_dimension=0, tiled=True)


def core_columns(values, core):
    size = lax.axis_size("z")
    width = values.shape[1] // (2 * size)
    return jnp.concatenate(
        [
            lax.dynamic_slice_in_dim(values, (2 * i + core) * width, width, axis=1)
            for i in range(size)
        ],
        axis=1,
    )


def far_core(left_side, right_side):
    return core_product(left_side, right_side, 1 - lax.axis_index("c"))


def to_core(product, pieces):
    return [lax.ppermute(piece, "c", SWAP) for piece in jnp.split(product, pieces)]


def near_core(left_side, right_side, sent):
    return core_product(left_side, right_side, lax.axis_index("c"), sent)


def back_start(pair):
    rows = pair.shape[0] // 2
    upper, lower = pair[:rows], pair[rows:]
    straight = lax.axis_index("y") == 0
    first = lax.ppermute(jnp.where(straight, upper, lower), ("y", "c"), turned_back(False))
    second = lax.ppermute(jnp.where(straight, lower, upper), ("y", "c"), turned_back(True))
    return first, second


def back_end(first, second):
    straight = lax.axis_index("c") == 0
    return jnp.concatenate(
        [jnp.where(straight, first, second), jnp.where(straight, second, first)]
    )


def assemble(here, there, groups):
    rows = here.shape[0] // 2
    straight = lax.axis_index("x") == 0
    here = here[:rows], here[rows:]
    there = there[:rows], there[rows:]
    quarters = [jnp.where(straight, a, b) for a, b in zip(here, there)] + [
        jnp.where(straight, b, a) for a, b in zip(here, there)
    ]
    width = here[0].shape[1] // groups
    return jnp.concatenate(
        [q[:, g * width : (g + 1) * width] for g in range(groups) for q in quarters], axis=1
    ).astype(F32)


def norm_parts(values):
    center = jnp.mean(values, axis=-1, keepdims=True)
    centered = values - center
    variance = jnp.mean(centered * centered, axis=-1, keepdims=True)
    inverse = lax.rsqrt(variance + EPSILON)
    return (centered * inverse, inverse)


def norm_backward(slope, normed, inverse, gain_row):
    scaled = slope * gain_row
    first_mean = jnp.mean(scaled, axis=-1, keepdims=True)
    second_mean = jnp.mean(scaled * normed, axis=-1, keepdims=True)
    return inverse * (scaled - first_mean - normed * second_mean)


def rotary_tables(segment_all):
    length = segment_all.shape[1]
    places = jnp.arange(length)
    same_doc = segment_all[:, :, None] == segment_all[:, None, :]
    earlier = places[:, None] > places[None, :]
    position = jnp.sum(jnp.where(same_doc & earlier, 1.0, 0.0), axis=2).astype(F32)
    lane = jnp.arange(2 * HEAD_DIM) % HEAD_DIM
    frequency = jnp.exp((lane % (ROT // 2)).astype(F32) * (-2.0 * math.log(10000.0) / ROT))
    frequency = jnp.where(lane < ROT, frequency, 0.0)
    angles = position[:, :, None] * frequency
    sines = jnp.sin(angles)
    return (
        jnp.cos(angles),
        jnp.where(lane >= ROT // 2, sines, 0.0),
        jnp.where(lane < ROT // 2, -sines, 0.0),
    )


def rows_product(left_side, right_side):
    return jnp.dot(left_side, right_side, preferred_element_type=F32)


def last_product(left_side, right_side):
    return lax.dot_general(
        left_side, right_side, (((1,), (1,)), ((), ())), preferred_element_type=F32
    )


def first_product(left_side, right_side):
    return lax.dot_general(
        left_side, right_side, (((0,), (0,)), ((), ())), preferred_element_type=F32
    )


def turned(values, cosines, later, sooner):
    width = values.shape[1]
    copies = width // cosines.shape[1]
    wide = [jnp.concatenate([t] * copies, axis=1) for t in (cosines, later, sooner)]
    return (
        values * wide[0]
        + pltpu.roll(values, ROT // 2, 1) * wide[1]
        + pltpu.roll(values, width - ROT // 2, 1) * wide[2]
    )


def transposed_probs(queries, keys_all, allowed):
    scores = last_product(keys_all, queries) * HEAD_DIM ** (-0.5)
    scores = jnp.where(allowed, scores, -1e30)
    shifted = jnp.exp(scores - jnp.max(scores, axis=0, keepdims=True))
    return shifted * (1.0 / jnp.sum(shifted, axis=0, keepdims=True))


def allowed_pairs(segment_column, segment_row):
    length = segment_column.shape[0]
    source = lax.broadcasted_iota(jnp.int32, (length, length), 0)
    target = lax.broadcasted_iota(jnp.int32, (length, length), 1)
    return (segment_column == segment_row) & (source <= target)


def head(values, kind, h):
    start = kind * PART_D + h * HEAD_DIM
    return values[:, start : start + HEAD_DIM]


def sequence_rows(i, half):
    return (
        pl.ds(pl.multiple_of((i + 2 * (i // 2)) * half, half), half),
        pl.ds(pl.multiple_of((2 + 4 * (i % 2) + i // 2) * half, half), half),
    )


def read_rows(ref, places):
    return jnp.concatenate([ref[place] for place in places])


def write_rows(ref, places, value):
    half = value.shape[0] // 2
    ref[places[0]] = value[:half]
    ref[places[1]] = value[half:]


def attend_kernel(
    joined_ref, bias_ref, cos_ref, later_ref, sooner_ref, column_ref, row_ref, qkv_ref, out_ref
):
    count, _, rows = row_ref.shape

    @pl.loop(0, count)
    def _(i):
        places = sequence_rows(i, rows // 2)
        joined = read_rows(joined_ref, places) + bias_ref[...]
        tables = (cos_ref[i], later_ref[i], sooner_ref[i])
        qkv = jnp.concatenate(
            [
                turned(joined[:, :PART_D], *tables).astype(BF16),
                turned(joined[:, PART_D : 2 * PART_D], *tables).astype(BF16),
                joined[:, 2 * PART_D :].astype(BF16),
            ],
            axis=1,
        )
        qkv_ref[i] = qkv
        allowed = allowed_pairs(column_ref[i], row_ref[i])
        heads = []
        for h in range(PART_HEADS):
            weights = transposed_probs(head(qkv, 0, h), head(qkv, 1, h), allowed).astype(BF16)
            heads.append(first_product(weights, head(qkv, 2, h)))
        write_rows(out_ref, places, jnp.concatenate(heads, axis=1).astype(BF16))


def attend_back_kernel(
    qkv_ref, slope_ref, cos_ref, later_ref, sooner_ref, column_ref, row_ref, out_ref, bias_ref
):
    count, _, rows = row_ref.shape
    bias_ref[...] = jnp.zeros_like(bias_ref)

    @pl.loop(0, count)
    def _(i):
        places = sequence_rows(i, rows // 2)
        qkv, slope = qkv_ref[i], read_rows(slope_ref, places)
        tables = (cos_ref[i], -later_ref[i], -sooner_ref[i])
        allowed = allowed_pairs(column_ref[i], row_ref[i])
        slope_queries, slope_keys, slope_values = [], [], []
        for h in range(PART_HEADS):
            queries, keys_all, values_all = (head(qkv, kind, h) for kind in range(3))
            slope_here = head(slope, 0, h)
            probs = transposed_probs(queries, keys_all, allowed)
            slope_values.append(rows_product(probs.astype(BF16), slope_here))
            slope_weights = last_product(values_all, slope_here)
            inner = jnp.sum(probs * slope_weights, axis=0, keepdims=True)
            slope_scores = (probs * (slope_weights - inner)).astype(BF16)
            slope_keys.append(rows_product(slope_scores, queries) * HEAD_DIM ** (-0.5))
            slope_queries.append(first_product(slope_scores, keys_all) * HEAD_DIM ** (-0.5))
        joined = jnp.concatenate(
            [
                turned(jnp.concatenate(slope_queries, axis=1), *tables).astype(BF16),
                turned(jnp.concatenate(slope_keys, axis=1), *tables).astype(BF16),
                jnp.concatenate(slope_values, axis=1).astype(BF16),
            ],
            axis=1,
        )
        write_rows(out_ref, places, joined)
        bias_ref[...] += jnp.sum(joined.astype(F32), axis=0, keepdims=True)


def core_kernel(core_ref, left_ref, right_ref, *rest):
    product = first_product(left_ref[...], right_ref[...])
    out_ref = rest[-1]
    if len(rest) == 1:
        out_ref[...] = product.astype(BF16)
    width = out_ref.shape[0]
    starts = [(ref, at) for ref in rest[:-1] for at in range(0, ref.shape[0], width)]
    for step, (ref, at) in enumerate(starts):

        @pl.when(pl.program_id(0) == step)
        def _():
            out_ref[...] = (product + ref[pl.ds(at, width)].astype(F32)).astype(BF16)


def core_product(left_side, right_side, core, sent=None):
    steps = lax.axis_size("z")
    (tokens, features), count = left_side.shape, right_side.shape[1]
    width = features // (2 * steps)
    if width % 128:
        product = first_product(core_columns(left_side, core), right_side)
        if sent is not None:
            product = product + jnp.concatenate(sent).astype(F32)
        return product.astype(BF16)
    sent = sent or []
    whole = [
        pl.BlockSpec(piece.shape, lambda i, core: (0, 0), pipeline_mode=pl.Buffered(1))
        for piece in sent
    ]
    return pl.pallas_call(
        core_kernel,
        grid_spec=pltpu.PrefetchScalarGridSpec(
            num_scalar_prefetch=1,
            grid=(steps,),
            in_specs=[
                pl.BlockSpec((tokens, width), lambda i, core: (0, 2 * i + core[0])),
                pl.BlockSpec(
                    (tokens, count), lambda i, core: (0, 0), pipeline_mode=pl.Buffered(1)
                ),
            ]
            + whole,
            out_specs=pl.BlockSpec((width, count), lambda i, core: (i, 0)),
        ),
        out_shape=jax.ShapeDtypeStruct((features // 2, count), BF16),
        compiler_params=pltpu.CompilerParams(vmem_limit_bytes=40 * 2**20),
        cost_estimate=NO_COST,
    )(core[None].astype(jnp.int32), left_side, right_side, *sent)


def plain_kernel(left_ref, right_ref, out_ref):
    out_ref[...] = rows_product(left_ref[...], right_ref[...]).astype(out_ref.dtype)


def column_product(left_side, right_side, column, count, dtype):
    tokens, depth = left_side.shape
    rows = tokens // 2
    return pl.pallas_call(
        plain_kernel,
        grid=(2,),
        in_specs=[
            pl.BlockSpec((rows, depth), lambda i: (i, 0)),
            pl.BlockSpec((depth, count), lambda i: (0, column), pipeline_mode=pl.Buffered(1)),
        ],
        out_specs=pl.BlockSpec((rows, count), lambda i: (i, 0)),
        out_shape=jax.ShapeDtypeStruct((tokens, count), dtype),
        compiler_params=pltpu.CompilerParams(vmem_limit_bytes=40 * 2**20),
        cost_estimate=NO_COST,
    )(left_side, right_side)


def far_kernel(left_ref, right_ref, out_ref):
    out_ref[...] = last_product(left_ref[...], right_ref[...]).astype(out_ref.dtype)


def half_product(left_side, half, right_side, column, dtype):
    rows, depth = left_side.shape[0] // 2, left_side.shape[1]
    count = right_side.shape[0]
    tile = min(count, 256)
    return pl.pallas_call(
        far_kernel,
        grid=(count // tile,),
        in_specs=[
            pl.BlockSpec((rows, depth), lambda i: (half, 0)),
            pl.BlockSpec((tile, depth), lambda i: (i, column)),
        ],
        out_specs=pl.BlockSpec((rows, tile), lambda i: (0, i)),
        out_shape=jax.ShapeDtypeStruct((rows, count), dtype),
        compiler_params=pltpu.CompilerParams(vmem_limit_bytes=40 * 2**20),
        cost_estimate=NO_COST,
    )(left_side, right_side)


def slope_kernel(cotangent_ref, weight_ref, gate_ref, up_ref, out_ref):
    width = weight_ref.shape[1]
    for start in range(0, width, 256):
        here = pl.ds(start, min(256, width - start))
        slope = rows_product(cotangent_ref[...], weight_ref[:, here])
        gate, up = gate_ref[:, here], up_ref[:, here]
        sigmoid = 1.0 / (1.0 + jnp.exp(-gate))
        swish = gate * sigmoid
        out_ref[:, here] = (slope * up * (sigmoid * (1.0 + gate * (1.0 - sigmoid)))).astype(BF16)
        out_ref[:, pl.ds(width + start, here.size)] = (slope * swish).astype(BF16)


def slopes_of_gate_up(cotangent_all, weight, gate_up):
    (tokens, features), width = cotangent_all.shape, weight.shape[1]
    rows = tokens // 2
    return pl.pallas_call(
        slope_kernel,
        grid=(2,),
        in_specs=[
            pl.BlockSpec((rows, features), lambda i: (i, 0)),
            pl.BlockSpec((features, width), lambda i: (0, 0), pipeline_mode=pl.Buffered(1)),
            pl.BlockSpec((rows, width), lambda i: (i, 0)),
            pl.BlockSpec((rows, width), lambda i: (i, 1)),
        ],
        out_specs=pl.BlockSpec((rows, 2 * width), lambda i: (i, 0)),
        out_shape=jax.ShapeDtypeStruct((tokens, 2 * width), BF16),
        compiler_params=pltpu.CompilerParams(vmem_limit_bytes=48 * 2**20),
        cost_estimate=NO_COST,
    )(cotangent_all, weight, gate_up, gate_up)


def in_vmem(count):
    return [pl.BlockSpec(memory_space=pltpu.VMEM)] * count


def attend(joined, bias, tables, segment_all):
    count, rows = segment_all.shape
    return pl.pallas_call(
        attend_kernel,
        in_specs=in_vmem(7),
        out_specs=in_vmem(2),
        out_shape=[
            jax.ShapeDtypeStruct((count, rows, 3 * PART_D), BF16),
            jax.ShapeDtypeStruct((count * rows, PART_D), BF16),
        ],
        compiler_params=pltpu.CompilerParams(vmem_limit_bytes=48 * 2**20),
        cost_estimate=NO_COST,
    )(joined, bias[None], *tables, segment_all[:, :, None], segment_all[:, None])


def attend_back(qkv, slope, tables, segment_all):
    count, rows = segment_all.shape
    joined, bias = pl.pallas_call(
        attend_back_kernel,
        in_specs=in_vmem(7),
        out_specs=in_vmem(2),
        out_shape=[
            jax.ShapeDtypeStruct((count * rows, 3 * PART_D), BF16),
            jax.ShapeDtypeStruct((1, 3 * PART_D), F32),
        ],
        compiler_params=pltpu.CompilerParams(vmem_limit_bytes=48 * 2**20),
        cost_estimate=NO_COST,
    )(qkv, slope, *tables, segment_all[:, :, None], segment_all[:, None])
    return joined, bias[0]


def after(values, *others):
    return lax.optimization_barrier((values, others))[0]


def in_order(axis, own, other):
    straight = lax.axis_index(axis) == 0
    return jnp.where(straight, jnp.concatenate([own, other]), jnp.concatenate([other, own]))


def all_z_start(block):
    size = lax.axis_size("z")
    return [
        lax.ppermute(block, "z", [(i, (i + step) % size) for i in range(size)])
        for step in range(1, size)
    ]


def all_z_end(block, arrived):
    size, z = lax.axis_size("z"), lax.axis_index("z")
    whole = jnp.stack([block, *arrived])[::-1].astype(F32)
    return lax.dynamic_slice_in_dim(jnp.concatenate([whole, whole]), size - 1 - z, size, axis=0)


def small_sum(vector):
    z_size = lax.axis_size("z")
    for axis in ("c", "y", "x"):
        vector = vector + lax.ppermute(vector, axis, SWAP)
    step = 1
    while step < z_size:
        vector = vector + lax.ppermute(vector, "z", [(i, i ^ step) for i in range(z_size)])
        step *= 2
    return vector


def shards(
    tokens,
    segments,
    attend_weight,
    attend_bias,
    output_weight,
    attend_gain,
    attend_shift,
    expand_weight,
    shrink_weight,
    dense_gain,
    dense_shift,
    cotangent,
):
    x, y = lax.axis_index("x"), lax.axis_index("y")
    part = 2 * x + y

    vectors = [attend_bias, attend_gain, attend_shift, dense_gain, dense_shift]
    small = jnp.concatenate(vectors)[None]
    turned_first = turn_start((attend_weight, 3), (output_weight, 1))
    arrived = lax.ppermute(small, "c", SWAP), over_x(segments)
    turned_first, arrived = after((turned_first, arrived))

    attend_and_output = gather_pair(turn_end(*turned_first))
    attend_all = attend_and_output[:, : 3 * PART_D]
    small = in_order("c", small, arrived[0])
    segment_all = jnp.concatenate([segments, arrived[1]])
    tokens, small, segment_all = after((tokens, small, segment_all), turned_first)
    tokens_near = near_start(tokens)
    arrived = over_y(small), over_y(segment_all)
    tokens_near, arrived = after((tokens_near, arrived))

    tokens_near = near_end(tokens, tokens_near)
    small = in_order("y", small, arrived[0])
    segment_all = jnp.concatenate([segment_all, arrived[1]])
    tables = rotary_tables(segment_all)
    tokens_far = gather_far(tokens_near)
    turned_next = turn_start((after(expand_weight, tokens_near), 2))
    arrived = all_z_start(small)
    tokens_far, turned_next, arrived = after((tokens_far, turned_next, arrived))

    expand_all = gather_pair(turn_end(*turned_next))
    cotangent_near = near_start(after(cotangent, turned_next))
    turned_next = turn_start((after(shrink_weight, turned_next), 1))
    small = all_z_end(small, arrived)
    bounds = [0]
    for v in vectors:
        bounds.append(bounds[-1] + v.shape[0])
    bias_full, gain_one, shift_one, gain_two, shift_two = [
        small[:, :, i:j].reshape(-1) for i, j in zip(bounds, bounds[1:])
    ]
    bias_part = lax.dynamic_index_in_dim(
        bias_full.reshape(3, PARTS, PART_D), part, axis=1, keepdims=False
    ).reshape(-1)
    token_all = jnp.concatenate([*tokens_near, *tokens_far])
    normed_all, _ = norm_parts(token_all.astype(F32))
    attend_input = (normed_all * gain_one + shift_one).astype(BF16)

    joined = rows_product(attend_input, attend_all)
    cotangent_near, turned_next = after((cotangent_near, turned_next), joined)
    shrink_all = gather_pair(turn_end(*turned_next))
    cotangent_near = near_end(cotangent, cotangent_near)
    qkv, attended = attend(joined, bias_part, tables, segment_all)
    start_rows = tokens.astype(F32)
    count = attended.shape[0] // 2
    far = half_product(attended, 1, attend_and_output, 3, BF16)
    sent = scatter_first(far)
    near = half_product(after(attended, far), 0, attend_and_output, 3, F32)
    sent = after(sent, near)
    middle = start_rows + scatter_end(*scatter_second(near, sent))
    normed_two, inverse_two = norm_parts(middle)
    dense_input = gather_tokens((normed_two * gain_two + shift_two).astype(BF16))
    cotangent_far = gather_far(after(cotangent_near, dense_input))
    gate_up = rows_product(dense_input, expand_all)
    gate_part = gate_up[:, :PART_FF]
    up_part = gate_up[:, PART_FF:]
    sigmoid_gate = jax.nn.sigmoid(gate_part)
    swish_gate = gate_part * sigmoid_gate
    hidden = (swish_gate * up_part).astype(BF16)
    cotangent_far, hidden = after((cotangent_far, hidden))
    cotangent_all = jnp.concatenate([*cotangent_near, *cotangent_far])

    core_sent = to_core(far_core(cotangent_all, hidden), CORE_PIECES)
    shrink_partial = near_core(cotangent_all, hidden, core_sent)
    shrink_slopes = scatter_pair(shrink_partial)
    slope_gate_up = slopes_of_gate_up(after(cotangent_all, shrink_partial), shrink_all, gate_up)
    expand_far = far_core(dense_input, slope_gate_up)
    core_sent = to_core(expand_far, CORE_PIECES)
    far = half_product(after(slope_gate_up, expand_far), 1, expand_all, 0, BF16)
    sent = scatter_first(far)
    near = half_product(after(slope_gate_up, far), 0, expand_all, 0, F32)
    expand_partial = near_core(dense_input, after(slope_gate_up, near), core_sent)
    expand_partial, shrink_slopes = after((expand_partial, shrink_slopes))
    expand_slopes = scatter_pair(expand_partial)
    sent = after(sent, expand_partial)
    last = scatter_second(near, sent)
    slope_dense = scatter_end(*last)
    dense_gain_part = jnp.sum(slope_dense * normed_two, axis=0)
    dense_shift_part = jnp.sum(slope_dense, axis=0)
    slope_middle = cotangent.astype(F32) + norm_backward(
        slope_dense, normed_two, inverse_two, gain_two
    )
    slope_branch = slope_middle.astype(BF16)
    branch_near = near_start(slope_branch)
    output_far = half_product(after(hidden, slope_branch), 1, shrink_all, 0, BF16)
    branch_near = near_end(slope_branch, after(branch_near, output_far))
    branch_far = gather_far(branch_near)
    output_near = half_product(after(hidden, branch_near), 0, shrink_all, 0, F32)
    slope_branch = jnp.concatenate([*branch_near, *after(branch_far, output_near)])
    output_far, shrink_slopes = after((output_far, shrink_slopes), slope_branch)
    output_sent = scatter_first(output_far)
    shrink_turn = back_start(shrink_slopes)
    slope_attended = column_product(slope_branch, attend_and_output, 3, PART_D, BF16)
    slope_joined, bias_slope = attend_back(qkv, slope_attended, tables, segment_all)
    slope_joined, output_sent, shrink_turn = after((slope_joined, output_sent, shrink_turn))
    attend_far = far_core(attend_input, slope_joined)
    core_sent = to_core(attend_far, 1)
    far = half_product(after(slope_joined, attend_far), 1, attend_and_output, 0, BF16)
    sent = scatter_first(far)
    attend_partial = near_core(attend_input, after(slope_joined, far), core_sent)
    attend_partial, expand_slopes = after((attend_partial, expand_slopes))
    attend_slopes = scatter_pair(attend_partial)
    output_sent, shrink_turn = after((output_sent, shrink_turn), attend_partial)
    output_last = scatter_second(output_near, output_sent)
    shrink_here = back_end(*shrink_turn)
    shrink_there = over_x(shrink_here)
    near = half_product(after(slope_joined, attend_partial), 0, attend_and_output, 0, F32)
    sent, output_last, shrink_there = after((sent, output_last, shrink_there), near)
    layer_output = (middle + scatter_end(*output_last)).astype(BF16)
    last = scatter_second(near, sent)
    expand_turn = back_start(after(expand_slopes, near))
    output_core = far_core(after(slope_branch, near), attended)
    core_sent = to_core(output_core, 1)
    last, expand_turn, core_sent = after((last, expand_turn, core_sent), output_core)
    output_slopes = scatter_pair(near_core(slope_branch, attended, core_sent))
    expand_here = back_end(*expand_turn)
    expand_there = over_x(expand_here)
    shrink_gradient = assemble(shrink_here, shrink_there, 1)
    slope_input = scatter_end(*last)
    normed_one, inverse_one = norm_parts(start_rows)
    attend_gain_part = jnp.sum(slope_input * normed_one, axis=0)
    attend_shift_part = jnp.sum(slope_input, axis=0)
    tokens_gradient = (
        slope_middle + norm_backward(slope_input, normed_one, inverse_one, gain_one)
    ).astype(BF16)
    attend_slopes, expand_there = after((attend_slopes, expand_there), tokens_gradient)
    attend_turn = back_start(attend_slopes)
    expand_gradient = assemble(expand_here, expand_there, 2)
    attend_turn = after(attend_turn, expand_gradient)
    attend_here = back_end(*attend_turn)
    rows = attend_here.shape[0] // 2
    attend_there = over_x(attend_here[:rows])
    attend_there, output_slopes = after((attend_there, output_slopes))
    output_turn = back_start(output_slopes)
    attend_there = jnp.concatenate([attend_there, over_x(attend_here[rows:])])
    output_here = back_end(*output_turn)
    output_there = over_x(output_here)
    attend_gradient = assemble(attend_here, attend_there, 3)
    output_gradient = assemble(output_here, output_there, 1)

    bias_wide = lax.dynamic_update_slice(
        jnp.zeros((3, PARTS, PART_D), F32), bias_slope.reshape(3, 1, PART_D), (0, part, 0)
    ).reshape(-1)
    small = [bias_wide, attend_gain_part, attend_shift_part, dense_gain_part, dense_shift_part]
    total = small_sum(jnp.concatenate(small))
    index = (lax.axis_index("z") * 2 + y) * 2 + lax.axis_index("c")
    owned, at = [], 0
    for vector, own in zip(small, (attend_bias, attend_gain, attend_shift, dense_gain, dense_shift)):
        size = own.shape[0]
        owned.append(lax.dynamic_slice_in_dim(total, at + index * size, size))
        at += vector.shape[0]
    return (
        layer_output,
        tokens_gradient,
        attend_gradient,
        owned[0],
        output_gradient,
        owned[1],
        owned[2],
        expand_gradient,
        shrink_gradient,
        owned[3],
        owned[4],
    )


def solution(mesh):
    replicas, shard = mesh.shape["replica"], mesh.shape["shard"]
    cut = Mesh(mesh.devices.reshape(replicas, shard // 4, 2, 2), ("x", "z", "y", "c"))
    batch, owner = ("x", "z", "y", "c"), ("z", "y", "c")
    in_specs = (
        P(batch, None),
        P(batch, None),
        P(owner, None),
        P(owner),
        P(owner, None),
        P(owner),
        P(owner),
        P(owner, None),
        P(owner, None),
        P(owner),
        P(owner),
        P(batch, None),
    )
    out_specs = (
        P(batch, None),
        P(batch, None),
        P(owner, None),
        P(owner),
        P(owner, None),
        P(owner),
        P(owner),
        P(owner, None),
        P(owner, None),
        P(owner),
        P(owner),
    )
    return jax.shard_map(shards, mesh=cut, in_specs=in_specs, out_specs=out_specs, check_vma=False)
```

```python
import functools
import math

import jax
import jax.numpy as jnp
from jax import lax
from jax.experimental import pallas as pl
from jax.experimental.pallas import tpu as pltpu
from jax.sharding import Mesh
from jax.sharding import PartitionSpec as P

D = 2048
HEADS = 32
HEAD_DIM = 64
FF = 5632
ROT = 16
PARTS = 4
PART_HEADS = HEADS // PARTS
PART_D = D // PARTS
PART_FF = FF // PARTS

EPSILON = 1e-05
F32 = jnp.float32
BF16 = jnp.bfloat16
SWAP = [(0, 1), (1, 0)]
CORE_PIECES = 2
NO_COST = pl.CostEstimate(flops=0, bytes_accessed=0, transcendentals=0)


def over_x(value):
    return lax.ppermute(value, "x", SWAP)


def over_y(value):
    return lax.ppermute(value, "y", SWAP)


def near_start(block):
    half = block.shape[0] // 2
    return over_x(block[:half]), over_y(block[half:])


def near_end(block, arrived):
    half = block.shape[0] // 2
    return jnp.concatenate([block[:half], arrived[0]]), jnp.concatenate([block[half:], arrived[1]])


def gather_far(near):
    return over_y(near[0]), over_x(near[1])


def gather_tokens(block):
    near = near_end(block, near_start(block))
    return jnp.concatenate([*near, *gather_far(near)])


def scatter_first(far):
    half = far.shape[0] // 4
    return over_y(far[: 2 * half]), over_x(far[2 * half :])


def scatter_second(near, sent):
    half = near.shape[0] // 4
    low = near[: 2 * half] + sent[0].astype(F32)
    high = near[2 * half :] + sent[1].astype(F32)
    last = over_x(low[half:].astype(BF16)), over_y(high[half:].astype(BF16))
    return low[:half], high[:half], *last


def scatter_end(low, high, low_last, high_last):
    return jnp.concatenate([low + low_last.astype(F32), high + high_last.astype(F32)])


def scatter_product(left_side, right_side, product):
    count = left_side.shape[0] // 2
    far = product(left_side[count:], right_side)
    sent = scatter_first(far)
    near = product(after(left_side, far)[:count], right_side)
    return scatter_end(*scatter_second(near, after(sent, near)))


def transposed(flip):
    pairs = [(y * 2 + c, (1 - c if flip else c) * 2 + y) for y in range(2) for c in range(2)]
    return [pair for pair in pairs if pair[0] != pair[1]]


def with_own(own, arrived):
    return jnp.where(lax.axis_index("y") == lax.axis_index("c"), own, arrived)


def turned_back(flip):
    return [(target, source) for source, target in transposed(flip)]


def columns(weight, groups, part):
    width = weight.shape[1] // (groups * PARTS)
    return jnp.concatenate(
        [
            lax.dynamic_slice_in_dim(weight, (g * PARTS + part) * width, width, axis=1)
            for g in range(groups)
        ],
        axis=1,
    )


def turn_start(*weights_and_groups):
    x, c = lax.axis_index("x"), lax.axis_index("c")

    def part_of(part):
        return jnp.concatenate([columns(w, g, part) for w, g in weights_and_groups], axis=1)

    own = part_of(2 * x + c)
    first = lax.ppermute(own, ("y", "c"), transposed(False))
    second = lax.ppermute(part_of(2 * x + 1 - c), ("y", "c"), transposed(True))
    return own, first, second


def turn_end(own, first, second):
    first = with_own(own, first)
    straight = lax.axis_index("y") == 0
    return jnp.concatenate(
        [jnp.where(straight, first, second), jnp.where(straight, second, first)]
    )


def gather_pair(pair):
    return lax.all_gather(pair, ("z", "c"), axis=0, tiled=True)


def scatter_pair(partial):
    return lax.psum_scatter(partial, "z", scatter_dimension=0, tiled=True)


def core_columns(values, core):
    size = lax.axis_size("z")
    width = values.shape[1] // (2 * size)
    return jnp.concatenate(
        [
            lax.dynamic_slice_in_dim(values, (2 * i + core) * width, width, axis=1)
            for i in range(size)
        ],
        axis=1,
    )


def far_core(left_side, right_side):
    return core_product(left_side, right_side, 1 - lax.axis_index("c"))


def to_core(product, pieces):
    return [lax.ppermute(piece, "c", SWAP) for piece in jnp.split(product, pieces)]


def near_core(left_side, right_side, sent):
    return core_product(left_side, right_side, lax.axis_index("c"), sent)


def back_start(pair):
    rows = pair.shape[0] // 2
    upper, lower = pair[:rows], pair[rows:]
    straight = lax.axis_index("y") == 0
    own = jnp.where(straight, upper, lower)
    first = lax.ppermute(own, ("y", "c"), turned_back(False))
    second = lax.ppermute(jnp.where(straight, lower, upper), ("y", "c"), turned_back(True))
    return own, first, second


def back_end(own, first, second):
    first = with_own(own, first)
    straight = lax.axis_index("c") == 0
    return jnp.concatenate(
        [jnp.where(straight, first, second), jnp.where(straight, second, first)]
    )


def assemble(here, there, groups):
    rows = here.shape[0] // 2
    straight = lax.axis_index("x") == 0
    here = here[:rows], here[rows:]
    there = there[:rows], there[rows:]
    quarters = [jnp.where(straight, a, b) for a, b in zip(here, there)] + [
        jnp.where(straight, b, a) for a, b in zip(here, there)
    ]
    width = here[0].shape[1] // groups
    return jnp.concatenate(
        [q[:, g * width : (g + 1) * width] for g in range(groups) for q in quarters], axis=1
    ).astype(F32)


def norm_parts(values):
    center = jnp.mean(values, axis=-1, keepdims=True)
    centered = values - center
    variance = jnp.mean(centered * centered, axis=-1, keepdims=True)
    inverse = lax.rsqrt(variance + EPSILON)
    return (centered * inverse, inverse)


def norm_backward(slope, normed, inverse, gain_row):
    scaled = slope * gain_row
    first_mean = jnp.mean(scaled, axis=-1, keepdims=True)
    second_mean = jnp.mean(scaled * normed, axis=-1, keepdims=True)
    return inverse * (scaled - first_mean - normed * second_mean)


def rotary_tables(segment_all):
    length = segment_all.shape[1]
    places = jnp.arange(length)
    same_doc = segment_all[:, :, None] == segment_all[:, None, :]
    earlier = places[:, None] > places[None, :]
    position = jnp.sum(jnp.where(same_doc & earlier, 1.0, 0.0), axis=2).astype(F32)
    lane = jnp.arange(2 * HEAD_DIM) % HEAD_DIM
    frequency = jnp.exp((lane % (ROT // 2)).astype(F32) * (-2.0 * math.log(10000.0) / ROT))
    frequency = jnp.where(lane < ROT, frequency, 0.0)
    angles = position[:, :, None] * frequency
    sines = jnp.sin(angles)
    return (
        jnp.cos(angles),
        jnp.where(lane >= ROT // 2, sines, 0.0),
        jnp.where(lane < ROT // 2, -sines, 0.0),
    )


def rows_product(left_side, right_side):
    return jnp.dot(left_side, right_side, preferred_element_type=F32)


def last_product(left_side, right_side):
    return lax.dot_general(
        left_side, right_side, (((1,), (1,)), ((), ())), preferred_element_type=F32
    )


def first_product(left_side, right_side):
    return lax.dot_general(
        left_side, right_side, (((0,), (0,)), ((), ())), preferred_element_type=F32
    )


def turned(values, cosines, later, sooner):
    width = values.shape[1]
    copies = width // cosines.shape[1]
    wide = [jnp.concatenate([t] * copies, axis=1) for t in (cosines, later, sooner)]
    return (
        values * wide[0]
        + pltpu.roll(values, ROT // 2, 1) * wide[1]
        + pltpu.roll(values, width - ROT // 2, 1) * wide[2]
    )


def transposed_probs(queries, keys_all, allowed):
    scores = last_product(keys_all, queries) * HEAD_DIM ** (-0.5)
    scores = jnp.where(allowed, scores, -1e30)
    shifted = jnp.exp(scores - jnp.max(scores, axis=0, keepdims=True))
    return shifted * (1.0 / jnp.sum(shifted, axis=0, keepdims=True))


def allowed_pairs(segment_column, segment_row):
    length = segment_column.shape[0]
    source = lax.broadcasted_iota(jnp.int32, (length, length), 0)
    target = lax.broadcasted_iota(jnp.int32, (length, length), 1)
    return (segment_column == segment_row) & (source <= target)


def head(values, kind, h):
    start = kind * PART_D + h * HEAD_DIM
    return values[:, start : start + HEAD_DIM]


def sequence_rows(i, half):
    return (
        pl.ds(pl.multiple_of((i + 2 * (i // 2)) * half, half), half),
        pl.ds(pl.multiple_of((2 + 4 * (i % 2) + i // 2) * half, half), half),
    )


def read_rows(ref, places):
    return jnp.concatenate([ref[place] for place in places])


def write_rows(ref, places, value):
    half = value.shape[0] // 2
    ref[places[0]] = value[:half]
    ref[places[1]] = value[half:]


def attend_kernel(
    joined_ref, bias_ref, cos_ref, later_ref, sooner_ref, column_ref, row_ref, qkv_ref, out_ref
):
    count, _, rows = row_ref.shape

    @pl.loop(0, count)
    def _(i):
        places = sequence_rows(i, rows // 2)
        joined = read_rows(joined_ref, places) + bias_ref[...]
        tables = (cos_ref[i], later_ref[i], sooner_ref[i])
        qkv = jnp.concatenate(
            [
                turned(joined[:, :PART_D], *tables).astype(BF16),
                turned(joined[:, PART_D : 2 * PART_D], *tables).astype(BF16),
                joined[:, 2 * PART_D :].astype(BF16),
            ],
            axis=1,
        )
        qkv_ref[i] = qkv
        allowed = allowed_pairs(column_ref[i], row_ref[i])
        heads = []
        for h in range(PART_HEADS):
            weights = transposed_probs(head(qkv, 0, h), head(qkv, 1, h), allowed).astype(BF16)
            heads.append(first_product(weights, head(qkv, 2, h)))
        write_rows(out_ref, places, jnp.concatenate(heads, axis=1).astype(BF16))


def attend_back_kernel(
    qkv_ref, slope_ref, cos_ref, later_ref, sooner_ref, column_ref, row_ref, out_ref, bias_ref
):
    count, _, rows = row_ref.shape
    bias_ref[...] = jnp.zeros_like(bias_ref)

    @pl.loop(0, count)
    def _(i):
        places = sequence_rows(i, rows // 2)
        qkv, slope = qkv_ref[i], read_rows(slope_ref, places)
        tables = (cos_ref[i], -later_ref[i], -sooner_ref[i])
        allowed = allowed_pairs(column_ref[i], row_ref[i])
        slope_queries, slope_keys, slope_values = [], [], []
        for h in range(PART_HEADS):
            queries, keys_all, values_all = (head(qkv, kind, h) for kind in range(3))
            slope_here = head(slope, 0, h)
            probs = transposed_probs(queries, keys_all, allowed)
            slope_values.append(rows_product(probs.astype(BF16), slope_here))
            slope_weights = last_product(values_all, slope_here)
            inner = jnp.sum(probs * slope_weights, axis=0, keepdims=True)
            slope_scores = (probs * (slope_weights - inner)).astype(BF16)
            slope_keys.append(rows_product(slope_scores, queries) * HEAD_DIM ** (-0.5))
            slope_queries.append(first_product(slope_scores, keys_all) * HEAD_DIM ** (-0.5))
        joined = jnp.concatenate(
            [
                turned(jnp.concatenate(slope_queries, axis=1), *tables).astype(BF16),
                turned(jnp.concatenate(slope_keys, axis=1), *tables).astype(BF16),
                jnp.concatenate(slope_values, axis=1).astype(BF16),
            ],
            axis=1,
        )
        write_rows(out_ref, places, joined)
        bias_ref[...] += jnp.sum(joined.astype(F32), axis=0, keepdims=True)


def core_kernel(core_ref, left_ref, right_ref, *rest):
    product = first_product(left_ref[...], right_ref[...])
    out_ref = rest[-1]
    if len(rest) == 1:
        out_ref[...] = product.astype(BF16)
    width = out_ref.shape[0]
    starts = [(ref, at) for ref in rest[:-1] for at in range(0, ref.shape[0], width)]
    for step, (ref, at) in enumerate(starts):

        @pl.when(pl.program_id(0) == step)
        def _():
            out_ref[...] = (product + ref[pl.ds(at, width)].astype(F32)).astype(BF16)


def core_product(left_side, right_side, core, sent=None):
    steps = lax.axis_size("z")
    (tokens, features), count = left_side.shape, right_side.shape[1]
    width = features // (2 * steps)
    if width % 128:
        product = first_product(core_columns(left_side, core), right_side)
        if sent is not None:
            product = product + jnp.concatenate(sent).astype(F32)
        return product.astype(BF16)
    sent = sent or []
    whole = [
        pl.BlockSpec(piece.shape, lambda i, core: (0, 0), pipeline_mode=pl.Buffered(1))
        for piece in sent
    ]
    return pl.pallas_call(
        core_kernel,
        grid_spec=pltpu.PrefetchScalarGridSpec(
            num_scalar_prefetch=1,
            grid=(steps,),
            in_specs=[
                pl.BlockSpec((tokens, width), lambda i, core: (0, 2 * i + core[0])),
                pl.BlockSpec(
                    (tokens, count), lambda i, core: (0, 0), pipeline_mode=pl.Buffered(1)
                ),
            ]
            + whole,
            out_specs=pl.BlockSpec((width, count), lambda i, core: (i, 0)),
        ),
        out_shape=jax.ShapeDtypeStruct((features // 2, count), BF16),
        compiler_params=pltpu.CompilerParams(vmem_limit_bytes=40 * 2**20),
        cost_estimate=NO_COST,
    )(core[None].astype(jnp.int32), left_side, right_side, *sent)


def near_and_core_kernel(
    tiles, core_ref, left_ref, right_ref, other_ref, *refs
):
    step = pl.program_id(0)
    near_ref, out_ref = refs[-2:]
    width = out_ref.shape[0]

    @pl.when(step < tiles)
    def _():
        near_ref[...] = last_product(left_ref[pl.ds(0, near_ref.shape[0])], right_ref[...])

    starts = [(ref, at) for ref in refs[:-2] for at in range(0, ref.shape[0], width)]
    for k, (ref, at) in enumerate(starts):

        @pl.when(step == tiles + k)
        def _():
            product = first_product(other_ref[...], left_ref[...])
            out_ref[...] = (product + ref[pl.ds(at, width)].astype(F32)).astype(BF16)


def near_and_core(left_side, right_side, other, sent):
    steps = lax.axis_size("z")
    tokens, depth = left_side.shape
    features, count = other.shape[1], right_side.shape[0]
    width, tile = features // (2 * steps), min(count, 512)
    if width % 128:
        return half_product(left_side, 0, right_side, 0, F32), near_core(other, left_side, sent)
    tiles = count // tile
    once = pl.Buffered(1)
    near, own = pl.pallas_call(
        functools.partial(near_and_core_kernel, tiles),
        grid_spec=pltpu.PrefetchScalarGridSpec(
            num_scalar_prefetch=1,
            grid=(tiles + steps,),
            in_specs=[
                pl.BlockSpec((tokens, depth), lambda i, core: (0, 0), pipeline_mode=once),
                pl.BlockSpec((tile, depth), lambda i, core: (jnp.minimum(i, tiles - 1), 0)),
                pl.BlockSpec(
                    (tokens, width),
                    lambda i, core: (0, 2 * jnp.maximum(i - tiles, 0) + core[0]),
                ),
            ]
            + [
                pl.BlockSpec(piece.shape, lambda i, core: (0, 0), pipeline_mode=once)
                for piece in sent
            ],
            out_specs=[
                pl.BlockSpec(
                    (tokens // 2, tile), lambda i, core: (0, jnp.minimum(i, tiles - 1))
                ),
                pl.BlockSpec((width, depth), lambda i, core: (jnp.maximum(i - tiles, 0), 0)),
            ],
        ),
        out_shape=[
            jax.ShapeDtypeStruct((tokens // 2, count), F32),
            jax.ShapeDtypeStruct((features // 2, depth), BF16),
        ],
        compiler_params=pltpu.CompilerParams(vmem_limit_bytes=44 * 2**20),
        cost_estimate=NO_COST,
    )(lax.axis_index("c")[None].astype(jnp.int32), left_side, right_side, other, *sent)
    return near, own


def plain_kernel(left_ref, right_ref, out_ref):
    out_ref[...] = rows_product(left_ref[...], right_ref[...]).astype(out_ref.dtype)


def column_product(left_side, right_side, column, count, dtype):
    tokens, depth = left_side.shape
    rows = tokens // 2
    return pl.pallas_call(
        plain_kernel,
        grid=(2,),
        in_specs=[
            pl.BlockSpec((rows, depth), lambda i: (i, 0)),
            pl.BlockSpec((depth, count), lambda i: (0, column), pipeline_mode=pl.Buffered(1)),
        ],
        out_specs=pl.BlockSpec((rows, count), lambda i: (i, 0)),
        out_shape=jax.ShapeDtypeStruct((tokens, count), dtype),
        compiler_params=pltpu.CompilerParams(vmem_limit_bytes=40 * 2**20),
        cost_estimate=NO_COST,
    )(left_side, right_side)


def far_kernel(left_ref, right_ref, out_ref):
    out_ref[...] = last_product(left_ref[...], right_ref[...]).astype(out_ref.dtype)


def half_product(left_side, half, right_side, column, dtype):
    rows, depth = left_side.shape[0] // 2, left_side.shape[1]
    count = right_side.shape[0]
    tile = min(count, 512)
    return pl.pallas_call(
        far_kernel,
        grid=(count // tile,),
        in_specs=[
            pl.BlockSpec((rows, depth), lambda i: (half, 0)),
            pl.BlockSpec((tile, depth), lambda i: (i, column)),
        ],
        out_specs=pl.BlockSpec((rows, tile), lambda i: (0, i)),
        out_shape=jax.ShapeDtypeStruct((rows, count), dtype),
        compiler_params=pltpu.CompilerParams(vmem_limit_bytes=40 * 2**20),
        cost_estimate=NO_COST,
    )(left_side, right_side)


def slope_kernel(cotangent_ref, weight_ref, gate_ref, up_ref, out_ref):
    width = weight_ref.shape[1]
    for start in range(0, width, 256):
        here = pl.ds(start, min(256, width - start))
        slope = rows_product(cotangent_ref[...], weight_ref[:, here])
        gate, up = gate_ref[:, here], up_ref[:, here]
        sigmoid = 1.0 / (1.0 + jnp.exp(-gate))
        swish = gate * sigmoid
        out_ref[:, here] = (slope * up * (sigmoid * (1.0 + gate * (1.0 - sigmoid)))).astype(BF16)
        out_ref[:, pl.ds(width + start, here.size)] = (slope * swish).astype(BF16)


def slopes_of_gate_up(cotangent_all, weight, gate_up):
    (tokens, features), width = cotangent_all.shape, weight.shape[1]
    rows = tokens // 4
    return pl.pallas_call(
        slope_kernel,
        grid=(4,),
        in_specs=[
            pl.BlockSpec((rows, features), lambda i: (i, 0)),
            pl.BlockSpec((features, width), lambda i: (0, 0), pipeline_mode=pl.Buffered(1)),
            pl.BlockSpec((rows, width), lambda i: (i, 0)),
            pl.BlockSpec((rows, width), lambda i: (i, 1)),
        ],
        out_specs=pl.BlockSpec((rows, 2 * width), lambda i: (i, 0)),
        out_shape=jax.ShapeDtypeStruct((tokens, 2 * width), BF16),
        compiler_params=pltpu.CompilerParams(vmem_limit_bytes=48 * 2**20),
        cost_estimate=NO_COST,
    )(cotangent_all, weight, gate_up, gate_up)


def in_vmem(count):
    return [pl.BlockSpec(memory_space=pltpu.VMEM)] * count


def attend(joined, bias, tables, segment_all):
    count, rows = segment_all.shape
    return pl.pallas_call(
        attend_kernel,
        in_specs=in_vmem(7),
        out_specs=in_vmem(2),
        out_shape=[
            jax.ShapeDtypeStruct((count, rows, 3 * PART_D), BF16),
            jax.ShapeDtypeStruct((count * rows, PART_D), BF16),
        ],
        compiler_params=pltpu.CompilerParams(vmem_limit_bytes=48 * 2**20),
        cost_estimate=NO_COST,
    )(joined, bias[None], *tables, segment_all[:, :, None], segment_all[:, None])


def attend_back(qkv, slope, tables, segment_all):
    count, rows = segment_all.shape
    joined, bias = pl.pallas_call(
        attend_back_kernel,
        in_specs=in_vmem(7),
        out_specs=in_vmem(2),
        out_shape=[
            jax.ShapeDtypeStruct((count * rows, 3 * PART_D), BF16),
            jax.ShapeDtypeStruct((1, 3 * PART_D), F32),
        ],
        compiler_params=pltpu.CompilerParams(vmem_limit_bytes=48 * 2**20),
        cost_estimate=NO_COST,
    )(qkv, slope, *tables, segment_all[:, :, None], segment_all[:, None])
    return joined, bias[0]


def after(values, *others):
    return lax.optimization_barrier((values, others))[0]


def in_order(axis, own, other):
    straight = lax.axis_index(axis) == 0
    return jnp.where(straight, jnp.concatenate([own, other]), jnp.concatenate([other, own]))


def all_z_start(block):
    size = lax.axis_size("z")
    return [
        lax.ppermute(block, "z", [(i, (i + step) % size) for i in range(size)])
        for step in range(1, size)
    ]


def all_z_end(block, arrived):
    size, z = lax.axis_size("z"), lax.axis_index("z")
    whole = jnp.stack([block, *arrived])[::-1].astype(F32)
    return lax.dynamic_slice_in_dim(jnp.concatenate([whole, whole]), size - 1 - z, size, axis=0)


def small_sum(vector):
    z_size = lax.axis_size("z")
    for axis in ("c", "y"):
        vector = vector + lax.ppermute(vector, axis, SWAP)
    step = 1
    while step < z_size:
        vector = vector + lax.ppermute(vector, "z", [(i, i ^ step) for i in range(z_size)])
        step *= 2
    return vector + over_x(vector)


def shards(
    tokens,
    segments,
    attend_weight,
    attend_bias,
    output_weight,
    attend_gain,
    attend_shift,
    expand_weight,
    shrink_weight,
    dense_gain,
    dense_shift,
    cotangent,
):
    x, y = lax.axis_index("x"), lax.axis_index("y")
    part = 2 * x + y

    vectors = [attend_bias, attend_gain, attend_shift, dense_gain, dense_shift]
    small = jnp.concatenate(vectors)[None]
    turned_first = turn_start((attend_weight, 3), (output_weight, 1))
    arrived = lax.ppermute(small, "c", SWAP), over_x(segments)
    turned_first, arrived = after((turned_first, arrived))

    attend_and_output = gather_pair(turn_end(*turned_first))
    attend_all = attend_and_output[:, : 3 * PART_D]
    small = in_order("c", small, arrived[0])
    segment_all = jnp.concatenate([segments, arrived[1]])
    tokens, small, segment_all = after((tokens, small, segment_all), turned_first)
    tokens_near = near_start(tokens)
    arrived = over_y(small), over_y(segment_all)
    tokens_near, arrived = after((tokens_near, arrived))

    tokens_near = near_end(tokens, tokens_near)
    small = in_order("y", small, arrived[0])
    segment_all = jnp.concatenate([segment_all, arrived[1]])
    tables = rotary_tables(segment_all)
    tokens_far = gather_far(tokens_near)
    turned_next = turn_start((after(expand_weight, tokens_near), 2))
    arrived = all_z_start(small)
    tokens_far, turned_next, arrived = after((tokens_far, turned_next, arrived))

    expand_all = gather_pair(turn_end(*turned_next))
    cotangent_near = near_start(after(cotangent, turned_next))
    turned_next = turn_start((after(shrink_weight, turned_next), 1))
    small = all_z_end(small, arrived)
    bounds = [0]
    for v in vectors:
        bounds.append(bounds[-1] + v.shape[0])
    bias_full, gain_one, shift_one, gain_two, shift_two = [
        small[:, :, i:j].reshape(-1) for i, j in zip(bounds, bounds[1:])
    ]
    bias_part = lax.dynamic_index_in_dim(
        bias_full.reshape(3, PARTS, PART_D), part, axis=1, keepdims=False
    ).reshape(-1)
    token_all = jnp.concatenate([*tokens_near, *tokens_far])
    normed_all, _ = norm_parts(token_all.astype(F32))
    attend_input = (normed_all * gain_one + shift_one).astype(BF16)

    joined = rows_product(attend_input, attend_all)
    cotangent_near, turned_next = after((cotangent_near, turned_next), joined)
    shrink_all = gather_pair(turn_end(*turned_next))
    cotangent_near = near_end(cotangent, cotangent_near)
    qkv, attended = attend(joined, bias_part, tables, segment_all)
    start_rows = tokens.astype(F32)
    count = attended.shape[0] // 2
    far = half_product(attended, 1, attend_and_output, 3, BF16)
    sent = scatter_first(far)
    near = half_product(after(attended, far), 0, attend_and_output, 3, F32)
    sent = after(sent, near)
    middle = start_rows + scatter_end(*scatter_second(near, sent))
    normed_two, inverse_two = norm_parts(middle)
    dense_input = gather_tokens((normed_two * gain_two + shift_two).astype(BF16))
    cotangent_far = gather_far(after(cotangent_near, dense_input))
    gate_up = rows_product(dense_input, expand_all)
    gate_part = gate_up[:, :PART_FF]
    up_part = gate_up[:, PART_FF:]
    sigmoid_gate = jax.nn.sigmoid(gate_part)
    swish_gate = gate_part * sigmoid_gate
    hidden = (swish_gate * up_part).astype(BF16)
    cotangent_far, hidden = after((cotangent_far, hidden))
    cotangent_all = jnp.concatenate([*cotangent_near, *cotangent_far])

    core_sent = to_core(far_core(cotangent_all, hidden), CORE_PIECES)
    shrink_partial = near_core(cotangent_all, hidden, core_sent)
    shrink_slopes = scatter_pair(shrink_partial)
    slope_gate_up = slopes_of_gate_up(after(cotangent_all, shrink_partial), shrink_all, gate_up)
    expand_far = far_core(dense_input, slope_gate_up)
    core_sent = to_core(expand_far, CORE_PIECES)
    far = half_product(after(slope_gate_up, expand_far), 1, expand_all, 0, BF16)
    sent = scatter_first(far)
    near, expand_partial = near_and_core(
        after(slope_gate_up, far), expand_all, dense_input, core_sent
    )
    expand_partial, shrink_slopes = after((expand_partial, shrink_slopes))
    expand_slopes = scatter_pair(expand_partial)
    sent = after(sent, expand_partial)
    last = scatter_second(near, sent)
    slope_dense = scatter_end(*last)
    dense_gain_part = jnp.sum(slope_dense * normed_two, axis=0)
    dense_shift_part = jnp.sum(slope_dense, axis=0)
    slope_middle = cotangent.astype(F32) + norm_backward(
        slope_dense, normed_two, inverse_two, gain_two
    )
    slope_branch = slope_middle.astype(BF16)
    branch_near = near_start(slope_branch)
    output_far = half_product(after(hidden, slope_branch), 1, shrink_all, 0, BF16)
    branch_near = near_end(slope_branch, after(branch_near, output_far))
    branch_far = gather_far(branch_near)
    output_near = half_product(after(hidden, branch_near), 0, shrink_all, 0, F32)
    slope_branch = jnp.concatenate([*branch_near, *after(branch_far, output_near)])
    output_far, shrink_slopes = after((output_far, shrink_slopes), slope_branch)
    output_sent = scatter_first(output_far)
    shrink_turn = back_start(shrink_slopes)
    slope_attended = column_product(slope_branch, attend_and_output, 3, PART_D, BF16)
    slope_joined, bias_slope = attend_back(qkv, slope_attended, tables, segment_all)
    slope_joined, output_sent, shrink_turn = after((slope_joined, output_sent, shrink_turn))
    shrink_here = back_end(*shrink_turn)
    shrink_there = over_x(shrink_here)
    attend_far = far_core(attend_input, slope_joined)
    core_sent = to_core(attend_far, 1)
    far = half_product(after(slope_joined, attend_far), 1, attend_and_output, 0, BF16)
    far, expand_slopes, core_sent = after((far, expand_slopes, core_sent))
    expand_turn = back_start(expand_slopes)
    sent = scatter_first(far)
    attend_partial = near_core(attend_input, after(slope_joined, far), core_sent)
    attend_slopes = scatter_pair(attend_partial)
    near = half_product(after(slope_joined, attend_partial), 0, attend_and_output, 0, F32)
    sent, expand_turn, shrink_there, near = after((sent, expand_turn, shrink_there, near))
    last = scatter_second(near, sent)
    output_last = scatter_second(output_near, after(output_sent, near))
    expand_here = back_end(*expand_turn)
    expand_there = over_x(expand_here)
    output_core = far_core(after(slope_branch, near), attended)
    last, output_last = after((last, output_last), output_core)
    core_sent = to_core(output_core, 1)
    layer_output = (middle + scatter_end(*output_last)).astype(BF16)
    shrink_gradient = assemble(shrink_here, shrink_there, 1)
    output_partial = near_core(slope_branch, attended, core_sent)
    output_slopes = scatter_pair(output_partial)
    slope_input = scatter_end(*after(last, output_partial))
    normed_one, inverse_one = norm_parts(start_rows)
    attend_gain_part = jnp.sum(slope_input * normed_one, axis=0)
    attend_shift_part = jnp.sum(slope_input, axis=0)
    tokens_gradient = (
        slope_middle + norm_backward(slope_input, normed_one, inverse_one, gain_one)
    ).astype(BF16)
    attend_slopes, expand_there = after((attend_slopes, expand_there), tokens_gradient)
    attend_turn = back_start(attend_slopes)
    expand_gradient = assemble(expand_here, expand_there, 2)
    attend_turn = after(attend_turn, expand_gradient)
    attend_here = back_end(*attend_turn)
    rows = attend_here.shape[0] // 2
    attend_there = over_x(attend_here[:rows])
    attend_there, output_slopes = after((attend_there, output_slopes))
    output_turn = back_start(output_slopes)
    attend_there = jnp.concatenate([attend_there, over_x(attend_here[rows:])])
    output_here = back_end(*output_turn)
    output_there = over_x(output_here)
    attend_gradient = assemble(attend_here, attend_there, 3)
    output_gradient = assemble(output_here, output_there, 1)

    bias_wide = lax.dynamic_update_slice(
        jnp.zeros((3, PARTS, PART_D), F32), bias_slope.reshape(3, 1, PART_D), (0, part, 0)
    ).reshape(-1)
    small = [bias_wide, attend_gain_part, attend_shift_part, dense_gain_part, dense_shift_part]
    total = small_sum(jnp.concatenate(small))
    index = (lax.axis_index("z") * 2 + y) * 2 + lax.axis_index("c")
    owned, at = [], 0
    for vector, own in zip(small, (attend_bias, attend_gain, attend_shift, dense_gain, dense_shift)):
        size = own.shape[0]
        owned.append(lax.dynamic_slice_in_dim(total, at + index * size, size))
        at += vector.shape[0]
    return (
        layer_output,
        tokens_gradient,
        attend_gradient,
        owned[0],
        output_gradient,
        owned[1],
        owned[2],
        expand_gradient,
        shrink_gradient,
        owned[3],
        owned[4],
    )


def solution(mesh):
    replicas, shard = mesh.shape["replica"], mesh.shape["shard"]
    cut = Mesh(mesh.devices.reshape(replicas, shard // 4, 2, 2), ("x", "z", "y", "c"))
    batch, owner = ("x", "z", "y", "c"), ("z", "y", "c")
    in_specs = (
        P(batch, None),
        P(batch, None),
        P(owner, None),
        P(owner),
        P(owner, None),
        P(owner),
        P(owner),
        P(owner, None),
        P(owner, None),
        P(owner),
        P(owner),
        P(batch, None),
    )
    out_specs = (
        P(batch, None),
        P(batch, None),
        P(owner, None),
        P(owner),
        P(owner, None),
        P(owner),
        P(owner),
        P(owner, None),
        P(owner, None),
        P(owner),
        P(owner),
    )
    return jax.shard_map(shards, mesh=cut, in_specs=in_specs, out_specs=out_specs, check_vma=False)
```

```python
import functools
import math

import jax
import jax.numpy as jnp
from jax import lax
from jax.experimental import pallas as pl
from jax.experimental.pallas import tpu as pltpu
from jax.sharding import Mesh
from jax.sharding import PartitionSpec as P

D = 2048
HEADS = 32
HEAD_DIM = 64
FF = 5632
ROT = 16
PARTS = 4
PART_HEADS = HEADS // PARTS
PART_D = D // PARTS
PART_FF = FF // PARTS

EPSILON = 1e-05
F32 = jnp.float32
BF16 = jnp.bfloat16
SWAP = [(0, 1), (1, 0)]
CORE_PIECES = 2
NO_COST = pl.CostEstimate(flops=0, bytes_accessed=0, transcendentals=0)


def over_x(value):
    return lax.ppermute(value, "x", SWAP)


def over_y(value):
    return lax.ppermute(value, "y", SWAP)


def near_start(block):
    half = block.shape[0] // 2
    return over_x(block[:half]), over_y(block[half:])


def near_end(block, arrived):
    half = block.shape[0] // 2
    return jnp.concatenate([block[:half], arrived[0]]), jnp.concatenate([block[half:], arrived[1]])


def gather_far(near):
    return over_y(near[0]), over_x(near[1])


def gather_tokens(block):
    near = near_end(block, near_start(block))
    return jnp.concatenate([*near, *gather_far(near)])


def scatter_first(far):
    half = far.shape[0] // 4
    return over_y(far[: 2 * half]), over_x(far[2 * half :])


def scatter_second(near, sent):
    half = near.shape[0] // 4
    low = near[: 2 * half] + sent[0].astype(F32)
    high = near[2 * half :] + sent[1].astype(F32)
    last = over_x(low[half:].astype(BF16)), over_y(high[half:].astype(BF16))
    return low[:half], high[:half], *last


def scatter_end(low, high, low_last, high_last):
    return jnp.concatenate([low + low_last.astype(F32), high + high_last.astype(F32)])


def scatter_product(left_side, right_side, product):
    count = left_side.shape[0] // 2
    far = product(left_side[count:], right_side)
    sent = scatter_first(far)
    near = product(after(left_side, far)[:count], right_side)
    return scatter_end(*scatter_second(near, after(sent, near)))


def transposed(flip):
    pairs = [(y * 2 + c, (1 - c if flip else c) * 2 + y) for y in range(2) for c in range(2)]
    return [pair for pair in pairs if pair[0] != pair[1]]


def with_own(own, arrived):
    return jnp.where(lax.axis_index("y") == lax.axis_index("c"), own, arrived)


def turned_back(flip):
    return [(target, source) for source, target in transposed(flip)]


def columns(weight, groups, part):
    width = weight.shape[1] // (groups * PARTS)
    return jnp.concatenate(
        [
            lax.dynamic_slice_in_dim(weight, (g * PARTS + part) * width, width, axis=1)
            for g in range(groups)
        ],
        axis=1,
    )


def turn_start(*weights_and_groups):
    x, c = lax.axis_index("x"), lax.axis_index("c")

    def part_of(part):
        return jnp.concatenate([columns(w, g, part) for w, g in weights_and_groups], axis=1)

    own = part_of(2 * x + c)
    first = lax.ppermute(own, ("y", "c"), transposed(False))
    second = lax.ppermute(part_of(2 * x + 1 - c), ("y", "c"), transposed(True))
    return own, first, second


def turn_end(own, first, second):
    first = with_own(own, first)
    straight = lax.axis_index("y") == 0
    return jnp.concatenate(
        [jnp.where(straight, first, second), jnp.where(straight, second, first)]
    )


def gather_pair(pair):
    return lax.all_gather(pair, ("z", "c"), axis=0, tiled=True)


def scatter_pair(partial):
    return lax.psum_scatter(partial, "z", scatter_dimension=0, tiled=True)


def core_columns(values, core):
    size = lax.axis_size("z")
    width = values.shape[1] // (2 * size)
    return jnp.concatenate(
        [
            lax.dynamic_slice_in_dim(values, (2 * i + core) * width, width, axis=1)
            for i in range(size)
        ],
        axis=1,
    )


def far_core(left_side, right_side):
    return core_product(left_side, right_side, 1 - lax.axis_index("c"))


def to_core(product, pieces):
    return [lax.ppermute(piece, "c", SWAP) for piece in jnp.split(product, pieces)]


def near_core(left_side, right_side, sent):
    return core_product(left_side, right_side, lax.axis_index("c"), sent)


def back_start(pair):
    rows = pair.shape[0] // 2
    upper, lower = pair[:rows], pair[rows:]
    straight = lax.axis_index("y") == 0
    own = jnp.where(straight, upper, lower)
    first = lax.ppermute(own, ("y", "c"), turned_back(False))
    second = lax.ppermute(jnp.where(straight, lower, upper), ("y", "c"), turned_back(True))
    return own, first, second


def back_end(own, first, second):
    first = with_own(own, first)
    straight = lax.axis_index("c") == 0
    return jnp.concatenate(
        [jnp.where(straight, first, second), jnp.where(straight, second, first)]
    )


def assemble(here, there, groups):
    rows = here.shape[0] // 2
    straight = lax.axis_index("x") == 0
    here = here[:rows], here[rows:]
    there = there[:rows], there[rows:]
    quarters = [jnp.where(straight, a, b) for a, b in zip(here, there)] + [
        jnp.where(straight, b, a) for a, b in zip(here, there)
    ]
    width = here[0].shape[1] // groups
    return jnp.concatenate(
        [q[:, g * width : (g + 1) * width] for g in range(groups) for q in quarters], axis=1
    ).astype(F32)


def norm_parts(values):
    center = jnp.mean(values, axis=-1, keepdims=True)
    centered = values - center
    variance = jnp.mean(centered * centered, axis=-1, keepdims=True)
    inverse = lax.rsqrt(variance + EPSILON)
    return (centered * inverse, inverse)


def norm_backward(slope, normed, inverse, gain_row):
    scaled = slope * gain_row
    first_mean = jnp.mean(scaled, axis=-1, keepdims=True)
    second_mean = jnp.mean(scaled * normed, axis=-1, keepdims=True)
    return inverse * (scaled - first_mean - normed * second_mean)


def rotary_tables(segment_all):
    length = segment_all.shape[1]
    places = jnp.arange(length)
    same_doc = segment_all[:, :, None] == segment_all[:, None, :]
    earlier = places[:, None] > places[None, :]
    position = jnp.sum(jnp.where(same_doc & earlier, 1.0, 0.0), axis=2).astype(F32)
    lane = jnp.arange(2 * HEAD_DIM) % HEAD_DIM
    frequency = jnp.exp((lane % (ROT // 2)).astype(F32) * (-2.0 * math.log(10000.0) / ROT))
    frequency = jnp.where(lane < ROT, frequency, 0.0)
    angles = position[:, :, None] * frequency
    sines = jnp.sin(angles)
    return (
        jnp.cos(angles),
        jnp.where(lane >= ROT // 2, sines, 0.0),
        jnp.where(lane < ROT // 2, -sines, 0.0),
    )


def rows_product(left_side, right_side):
    return jnp.dot(left_side, right_side, preferred_element_type=F32)


def last_product(left_side, right_side):
    return lax.dot_general(
        left_side, right_side, (((1,), (1,)), ((), ())), preferred_element_type=F32
    )


def first_product(left_side, right_side):
    return lax.dot_general(
        left_side, right_side, (((0,), (0,)), ((), ())), preferred_element_type=F32
    )


def turned(values, cosines, later, sooner):
    width = values.shape[1]
    copies = width // cosines.shape[1]
    wide = [jnp.concatenate([t] * copies, axis=1) for t in (cosines, later, sooner)]
    return (
        values * wide[0]
        + pltpu.roll(values, ROT // 2, 1) * wide[1]
        + pltpu.roll(values, width - ROT // 2, 1) * wide[2]
    )


def transposed_probs(queries, keys_all, allowed):
    scores = last_product(keys_all, queries) * HEAD_DIM ** (-0.5)
    scores = jnp.where(allowed, scores, -1e30)
    shifted = jnp.exp(scores - jnp.max(scores, axis=0, keepdims=True))
    return shifted * (1.0 / jnp.sum(shifted, axis=0, keepdims=True))


def allowed_pairs(segment_column, segment_row):
    length = segment_column.shape[0]
    source = lax.broadcasted_iota(jnp.int32, (length, length), 0)
    target = lax.broadcasted_iota(jnp.int32, (length, length), 1)
    return (segment_column == segment_row) & (source <= target)


def head(values, kind, h):
    start = kind * PART_D + h * HEAD_DIM
    return values[:, start : start + HEAD_DIM]


def sequence_rows(i, half):
    return (
        pl.ds(pl.multiple_of((i + 2 * (i // 2)) * half, half), half),
        pl.ds(pl.multiple_of((2 + 4 * (i % 2) + i // 2) * half, half), half),
    )


def read_rows(ref, places):
    return jnp.concatenate([ref[place] for place in places])


def write_rows(ref, places, value):
    half = value.shape[0] // 2
    ref[places[0]] = value[:half]
    ref[places[1]] = value[half:]


def attend_kernel(
    joined_ref, bias_ref, cos_ref, later_ref, sooner_ref, column_ref, row_ref, qkv_ref, out_ref
):
    count, _, rows = row_ref.shape

    @pl.loop(0, count)
    def _(i):
        places = sequence_rows(i, rows // 2)
        joined = read_rows(joined_ref, places) + bias_ref[...]
        tables = (cos_ref[i], later_ref[i], sooner_ref[i])
        qkv = jnp.concatenate(
            [
                turned(joined[:, :PART_D], *tables).astype(BF16),
                turned(joined[:, PART_D : 2 * PART_D], *tables).astype(BF16),
                joined[:, 2 * PART_D :].astype(BF16),
            ],
            axis=1,
        )
        qkv_ref[i] = qkv
        allowed = allowed_pairs(column_ref[i], row_ref[i])
        heads = []
        for h in range(PART_HEADS):
            weights = transposed_probs(head(qkv, 0, h), head(qkv, 1, h), allowed).astype(BF16)
            heads.append(first_product(weights, head(qkv, 2, h)))
        write_rows(out_ref, places, jnp.concatenate(heads, axis=1).astype(BF16))


def attend_back_kernel(
    qkv_ref, slope_ref, cos_ref, later_ref, sooner_ref, column_ref, row_ref, out_ref, bias_ref
):
    count, _, rows = row_ref.shape
    bias_ref[...] = jnp.zeros_like(bias_ref)

    @pl.loop(0, count)
    def _(i):
        places = sequence_rows(i, rows // 2)
        qkv, slope = qkv_ref[i], read_rows(slope_ref, places)
        tables = (cos_ref[i], -later_ref[i], -sooner_ref[i])
        allowed = allowed_pairs(column_ref[i], row_ref[i])
        slope_queries, slope_keys, slope_values = [], [], []
        for h in range(PART_HEADS):
            queries, keys_all, values_all = (head(qkv, kind, h) for kind in range(3))
            slope_here = head(slope, 0, h)
            probs = transposed_probs(queries, keys_all, allowed)
            slope_values.append(rows_product(probs.astype(BF16), slope_here))
            slope_weights = last_product(values_all, slope_here)
            inner = jnp.sum(probs * slope_weights, axis=0, keepdims=True)
            slope_scores = (probs * (slope_weights - inner)).astype(BF16)
            slope_keys.append(rows_product(slope_scores, queries) * HEAD_DIM ** (-0.5))
            slope_queries.append(first_product(slope_scores, keys_all) * HEAD_DIM ** (-0.5))
        joined = jnp.concatenate(
            [
                turned(jnp.concatenate(slope_queries, axis=1), *tables).astype(BF16),
                turned(jnp.concatenate(slope_keys, axis=1), *tables).astype(BF16),
                jnp.concatenate(slope_values, axis=1).astype(BF16),
            ],
            axis=1,
        )
        write_rows(out_ref, places, joined)
        bias_ref[...] += jnp.sum(joined.astype(F32), axis=0, keepdims=True)


def core_kernel(core_ref, left_ref, right_ref, *rest):
    product = first_product(left_ref[...], right_ref[...])
    out_ref = rest[-1]
    if len(rest) == 1:
        out_ref[...] = product.astype(BF16)
    width = out_ref.shape[0]
    starts = [(ref, at) for ref in rest[:-1] for at in range(0, ref.shape[0], width)]
    for step, (ref, at) in enumerate(starts):

        @pl.when(pl.program_id(0) == step)
        def _():
            out_ref[...] = (product + ref[pl.ds(at, width)].astype(F32)).astype(BF16)


def core_product(left_side, right_side, core, sent=None):
    steps = lax.axis_size("z")
    (tokens, features), count = left_side.shape, right_side.shape[1]
    width = features // (2 * steps)
    if width % 128:
        product = first_product(core_columns(left_side, core), right_side)
        if sent is not None:
            product = product + jnp.concatenate(sent).astype(F32)
        return product.astype(BF16)
    sent = sent or []
    whole = [
        pl.BlockSpec(piece.shape, lambda i, core: (0, 0), pipeline_mode=pl.Buffered(1))
        for piece in sent
    ]
    return pl.pallas_call(
        core_kernel,
        grid_spec=pltpu.PrefetchScalarGridSpec(
            num_scalar_prefetch=1,
            grid=(steps,),
            in_specs=[
                pl.BlockSpec((tokens, width), lambda i, core: (0, 2 * i + core[0])),
                pl.BlockSpec(
                    (tokens, count), lambda i, core: (0, 0), pipeline_mode=pl.Buffered(1)
                ),
            ]
            + whole,
            out_specs=pl.BlockSpec((width, count), lambda i, core: (i, 0)),
        ),
        out_shape=jax.ShapeDtypeStruct((features // 2, count), BF16),
        compiler_params=pltpu.CompilerParams(vmem_limit_bytes=40 * 2**20),
        cost_estimate=NO_COST,
    )(core[None].astype(jnp.int32), left_side, right_side, *sent)


def near_and_core_kernel(
    tiles, core_ref, left_ref, right_ref, other_ref, *refs
):
    step = pl.program_id(0)
    near_ref, out_ref = refs[-2:]
    width = out_ref.shape[0]

    @pl.when(step < tiles)
    def _():
        near_ref[...] = last_product(left_ref[pl.ds(0, near_ref.shape[0])], right_ref[...])

    starts = [(ref, at) for ref in refs[:-2] for at in range(0, ref.shape[0], width)]
    for k, (ref, at) in enumerate(starts):

        @pl.when(step == tiles + k)
        def _():
            product = first_product(other_ref[...], left_ref[...])
            out_ref[...] = (product + ref[pl.ds(at, width)].astype(F32)).astype(BF16)


def near_and_core(left_side, right_side, other, sent):
    steps = lax.axis_size("z")
    tokens, depth = left_side.shape
    features, count = other.shape[1], right_side.shape[0]
    width, tile = features // (2 * steps), min(count, 512)
    if width % 128:
        return half_product(left_side, 0, right_side, 0, F32), near_core(other, left_side, sent)
    tiles = count // tile
    once = pl.Buffered(1)
    near, own = pl.pallas_call(
        functools.partial(near_and_core_kernel, tiles),
        grid_spec=pltpu.PrefetchScalarGridSpec(
            num_scalar_prefetch=1,
            grid=(tiles + steps,),
            in_specs=[
                pl.BlockSpec((tokens, depth), lambda i, core: (0, 0), pipeline_mode=once),
                pl.BlockSpec((tile, depth), lambda i, core: (jnp.minimum(i, tiles - 1), 0)),
                pl.BlockSpec(
                    (tokens, width),
                    lambda i, core: (0, 2 * jnp.maximum(i - tiles, 0) + core[0]),
                ),
            ]
            + [
                pl.BlockSpec(piece.shape, lambda i, core: (0, 0), pipeline_mode=once)
                for piece in sent
            ],
            out_specs=[
                pl.BlockSpec(
                    (tokens // 2, tile), lambda i, core: (0, jnp.minimum(i, tiles - 1))
                ),
                pl.BlockSpec((width, depth), lambda i, core: (jnp.maximum(i - tiles, 0), 0)),
            ],
        ),
        out_shape=[
            jax.ShapeDtypeStruct((tokens // 2, count), F32),
            jax.ShapeDtypeStruct((features // 2, depth), BF16),
        ],
        compiler_params=pltpu.CompilerParams(vmem_limit_bytes=44 * 2**20),
        cost_estimate=NO_COST,
    )(lax.axis_index("c")[None].astype(jnp.int32), left_side, right_side, other, *sent)
    return near, own


def plain_kernel(left_ref, right_ref, out_ref):
    out_ref[...] = rows_product(left_ref[...], right_ref[...]).astype(out_ref.dtype)


def column_product(left_side, right_side, column, count, dtype):
    tokens, depth = left_side.shape
    rows = tokens // 4
    return pl.pallas_call(
        plain_kernel,
        grid=(4,),
        in_specs=[
            pl.BlockSpec((rows, depth), lambda i: (i, 0)),
            pl.BlockSpec((depth, count), lambda i: (0, column), pipeline_mode=pl.Buffered(1)),
        ],
        out_specs=pl.BlockSpec((rows, count), lambda i: (i, 0)),
        out_shape=jax.ShapeDtypeStruct((tokens, count), dtype),
        compiler_params=pltpu.CompilerParams(vmem_limit_bytes=40 * 2**20),
        cost_estimate=NO_COST,
    )(left_side, right_side)


def far_kernel(left_ref, right_ref, out_ref):
    out_ref[...] = last_product(left_ref[...], right_ref[...]).astype(out_ref.dtype)


def half_product(left_side, half, right_side, column, dtype):
    rows, depth = left_side.shape[0] // 2, left_side.shape[1]
    count = right_side.shape[0]
    tile = min(count, 512 if depth > PART_FF else 1024)
    return pl.pallas_call(
        far_kernel,
        grid=(count // tile,),
        in_specs=[
            pl.BlockSpec((rows, depth), lambda i: (half, 0)),
            pl.BlockSpec((tile, depth), lambda i: (i, column)),
        ],
        out_specs=pl.BlockSpec((rows, tile), lambda i: (0, i)),
        out_shape=jax.ShapeDtypeStruct((rows, count), dtype),
        compiler_params=pltpu.CompilerParams(vmem_limit_bytes=40 * 2**20),
        cost_estimate=NO_COST,
    )(left_side, right_side)


def slope_kernel(cotangent_ref, weight_ref, gate_ref, up_ref, out_ref):
    width = weight_ref.shape[1]
    for start in range(0, width, 256):
        here = pl.ds(start, min(256, width - start))
        slope = rows_product(cotangent_ref[...], weight_ref[:, here])
        gate, up = gate_ref[:, here], up_ref[:, here]
        sigmoid = 1.0 / (1.0 + jnp.exp(-gate))
        swish = gate * sigmoid
        out_ref[:, here] = (slope * up * (sigmoid * (1.0 + gate * (1.0 - sigmoid)))).astype(BF16)
        out_ref[:, pl.ds(width + start, here.size)] = (slope * swish).astype(BF16)


def slopes_of_gate_up(cotangent_all, weight, gate_up):
    (tokens, features), width = cotangent_all.shape, weight.shape[1]
    rows = tokens // 4
    return pl.pallas_call(
        slope_kernel,
        grid=(4,),
        in_specs=[
            pl.BlockSpec((rows, features), lambda i: (i, 0)),
            pl.BlockSpec((features, width), lambda i: (0, 0), pipeline_mode=pl.Buffered(1)),
            pl.BlockSpec((rows, width), lambda i: (i, 0)),
            pl.BlockSpec((rows, width), lambda i: (i, 1)),
        ],
        out_specs=pl.BlockSpec((rows, 2 * width), lambda i: (i, 0)),
        out_shape=jax.ShapeDtypeStruct((tokens, 2 * width), BF16),
        compiler_params=pltpu.CompilerParams(vmem_limit_bytes=48 * 2**20),
        cost_estimate=NO_COST,
    )(cotangent_all, weight, gate_up, gate_up)


def in_vmem(count):
    return [pl.BlockSpec(memory_space=pltpu.VMEM)] * count


def attend(joined, bias, tables, segment_all):
    count, rows = segment_all.shape
    return pl.pallas_call(
        attend_kernel,
        in_specs=in_vmem(7),
        out_specs=in_vmem(2),
        out_shape=[
            jax.ShapeDtypeStruct((count, rows, 3 * PART_D), BF16),
            jax.ShapeDtypeStruct((count * rows, PART_D), BF16),
        ],
        compiler_params=pltpu.CompilerParams(vmem_limit_bytes=48 * 2**20),
        cost_estimate=NO_COST,
    )(joined, bias[None], *tables, segment_all[:, :, None], segment_all[:, None])


def attend_back(qkv, slope, tables, segment_all):
    count, rows = segment_all.shape
    joined, bias = pl.pallas_call(
        attend_back_kernel,
        in_specs=in_vmem(7),
        out_specs=in_vmem(2),
        out_shape=[
            jax.ShapeDtypeStruct((count * rows, 3 * PART_D), BF16),
            jax.ShapeDtypeStruct((1, 3 * PART_D), F32),
        ],
        compiler_params=pltpu.CompilerParams(vmem_limit_bytes=48 * 2**20),
        cost_estimate=NO_COST,
    )(qkv, slope, *tables, segment_all[:, :, None], segment_all[:, None])
    return joined, bias[0]


def after(values, *others):
    return lax.optimization_barrier((values, others))[0]


def in_order(axis, own, other):
    straight = lax.axis_index(axis) == 0
    return jnp.where(straight, jnp.concatenate([own, other]), jnp.concatenate([other, own]))


def all_z_start(block):
    size = lax.axis_size("z")
    return [
        lax.ppermute(block, "z", [(i, (i + step) % size) for i in range(size)])
        for step in range(1, size)
    ]


def all_z_end(block, arrived):
    size, z = lax.axis_size("z"), lax.axis_index("z")
    whole = jnp.stack([block, *arrived])[::-1].astype(F32)
    return lax.dynamic_slice_in_dim(jnp.concatenate([whole, whole]), size - 1 - z, size, axis=0)


def small_sum(vector):
    z_size = lax.axis_size("z")
    for axis in ("c", "y"):
        vector = vector + lax.ppermute(vector, axis, SWAP)
    step = 1
    while step < z_size:
        vector = vector + lax.ppermute(vector, "z", [(i, i ^ step) for i in range(z_size)])
        step *= 2
    return vector + over_x(vector)


def shards(
    tokens,
    segments,
    attend_weight,
    attend_bias,
    output_weight,
    attend_gain,
    attend_shift,
    expand_weight,
    shrink_weight,
    dense_gain,
    dense_shift,
    cotangent,
):
    x, y = lax.axis_index("x"), lax.axis_index("y")
    part = 2 * x + y

    vectors = [attend_bias, attend_gain, attend_shift, dense_gain, dense_shift]
    small = jnp.concatenate(vectors)[None]
    turned_first = turn_start((attend_weight, 3), (output_weight, 1))
    arrived = lax.ppermute(small, "c", SWAP), over_x(segments)
    turned_first, arrived = after((turned_first, arrived))

    attend_and_output = gather_pair(turn_end(*turned_first))
    attend_all = attend_and_output[:, : 3 * PART_D]
    small = in_order("c", small, arrived[0])
    segment_all = jnp.concatenate([segments, arrived[1]])
    tokens, small, segment_all = after((tokens, small, segment_all), turned_first)
    tokens_near = near_start(tokens)
    arrived = over_y(small), over_y(segment_all)
    tokens_near, arrived = after((tokens_near, arrived))

    tokens_near = near_end(tokens, tokens_near)
    small = in_order("y", small, arrived[0])
    segment_all = jnp.concatenate([segment_all, arrived[1]])
    tables = rotary_tables(segment_all)
    tokens_far = gather_far(tokens_near)
    turned_next = turn_start((after(expand_weight, tokens_near), 2))
    arrived = all_z_start(small)
    tokens_far, turned_next, arrived = after((tokens_far, turned_next, arrived))

    expand_all = gather_pair(turn_end(*turned_next))
    cotangent_near = near_start(after(cotangent, turned_next))
    turned_next = turn_start((after(shrink_weight, turned_next), 1))
    small = all_z_end(small, arrived)
    bounds = [0]
    for v in vectors:
        bounds.append(bounds[-1] + v.shape[0])
    bias_full, gain_one, shift_one, gain_two, shift_two = [
        small[:, :, i:j].reshape(-1) for i, j in zip(bounds, bounds[1:])
    ]
    bias_part = lax.dynamic_index_in_dim(
        bias_full.reshape(3, PARTS, PART_D), part, axis=1, keepdims=False
    ).reshape(-1)
    token_all = jnp.concatenate([*tokens_near, *tokens_far])
    normed_all, _ = norm_parts(token_all.astype(F32))
    attend_input = (normed_all * gain_one + shift_one).astype(BF16)

    joined = rows_product(attend_input, attend_all)
    cotangent_near, turned_next = after((cotangent_near, turned_next), joined)
    shrink_all = gather_pair(turn_end(*turned_next))
    cotangent_near = near_end(cotangent, cotangent_near)
    qkv, attended = attend(joined, bias_part, tables, segment_all)
    start_rows = tokens.astype(F32)
    count = attended.shape[0] // 2
    far = half_product(attended, 1, attend_and_output, 3, BF16)
    sent = scatter_first(far)
    near = half_product(after(attended, far), 0, attend_and_output, 3, F32)
    sent = after(sent, near)
    middle = start_rows + scatter_end(*scatter_second(near, sent))
    normed_two, inverse_two = norm_parts(middle)
    dense_input = gather_tokens((normed_two * gain_two + shift_two).astype(BF16))
    cotangent_far = gather_far(after(cotangent_near, dense_input))
    gate_up = rows_product(dense_input, expand_all)
    gate_part = gate_up[:, :PART_FF]
    up_part = gate_up[:, PART_FF:]
    sigmoid_gate = jax.nn.sigmoid(gate_part)
    swish_gate = gate_part * sigmoid_gate
    hidden = (swish_gate * up_part).astype(BF16)
    cotangent_far, hidden = after((cotangent_far, hidden))
    cotangent_all = jnp.concatenate([*cotangent_near, *cotangent_far])

    core_sent = to_core(far_core(cotangent_all, hidden), CORE_PIECES)
    shrink_partial = near_core(cotangent_all, hidden, core_sent)
    shrink_slopes = scatter_pair(shrink_partial)
    slope_gate_up = slopes_of_gate_up(after(cotangent_all, shrink_partial), shrink_all, gate_up)
    expand_far = far_core(dense_input, slope_gate_up)
    core_sent = to_core(expand_far, CORE_PIECES)
    far = half_product(after(slope_gate_up, expand_far), 1, expand_all, 0, BF16)
    sent = scatter_first(far)
    near, expand_partial = near_and_core(
        after(slope_gate_up, far), expand_all, dense_input, core_sent
    )
    expand_partial, shrink_slopes = after((expand_partial, shrink_slopes))
    expand_slopes = scatter_pair(expand_partial)
    sent = after(sent, expand_partial)
    last = scatter_second(near, sent)
    slope_dense = scatter_end(*last)
    dense_gain_part = jnp.sum(slope_dense * normed_two, axis=0)
    dense_shift_part = jnp.sum(slope_dense, axis=0)
    slope_middle = cotangent.astype(F32) + norm_backward(
        slope_dense, normed_two, inverse_two, gain_two
    )
    slope_branch = slope_middle.astype(BF16)
    branch_near = near_start(slope_branch)
    output_far = half_product(after(hidden, slope_branch), 1, shrink_all, 0, BF16)
    branch_near = near_end(slope_branch, after(branch_near, output_far))
    branch_far = gather_far(branch_near)
    output_near = half_product(after(hidden, branch_near), 0, shrink_all, 0, F32)
    slope_branch = jnp.concatenate([*branch_near, *after(branch_far, output_near)])
    output_far, shrink_slopes = after((output_far, shrink_slopes), slope_branch)
    output_sent = scatter_first(output_far)
    shrink_turn = back_start(shrink_slopes)
    slope_attended = column_product(slope_branch, attend_and_output, 3, PART_D, BF16)
    slope_joined, bias_slope = attend_back(qkv, slope_attended, tables, segment_all)
    slope_joined, output_sent, shrink_turn = after((slope_joined, output_sent, shrink_turn))
    shrink_here = back_end(*shrink_turn)
    shrink_there = over_x(shrink_here)
    attend_far = far_core(attend_input, slope_joined)
    core_sent = to_core(attend_far, 1)
    far = half_product(after(slope_joined, attend_far), 1, attend_and_output, 0, BF16)
    far, expand_slopes, core_sent = after((far, expand_slopes, core_sent))
    expand_turn = back_start(expand_slopes)
    sent = scatter_first(far)
    attend_partial = near_core(attend_input, after(slope_joined, far), core_sent)
    attend_slopes = scatter_pair(attend_partial)
    near = half_product(after(slope_joined, attend_partial), 0, attend_and_output, 0, F32)
    sent, expand_turn, shrink_there, near = after((sent, expand_turn, shrink_there, near))
    last = scatter_second(near, sent)
    output_last = scatter_second(output_near, after(output_sent, near))
    expand_here = back_end(*expand_turn)
    expand_there = over_x(expand_here)
    output_core = far_core(after(slope_branch, near), attended)
    last, output_last = after((last, output_last), output_core)
    core_sent = to_core(output_core, 1)
    layer_output = (middle + scatter_end(*output_last)).astype(BF16)
    shrink_gradient = assemble(shrink_here, shrink_there, 1)
    output_partial = near_core(slope_branch, attended, core_sent)
    output_slopes = scatter_pair(output_partial)
    slope_input = scatter_end(*after(last, output_partial))
    normed_one, inverse_one = norm_parts(start_rows)
    attend_gain_part = jnp.sum(slope_input * normed_one, axis=0)
    attend_shift_part = jnp.sum(slope_input, axis=0)
    tokens_gradient = (
        slope_middle + norm_backward(slope_input, normed_one, inverse_one, gain_one)
    ).astype(BF16)
    attend_slopes, expand_there = after((attend_slopes, expand_there), tokens_gradient)
    attend_turn = back_start(attend_slopes)
    expand_gradient = assemble(expand_here, expand_there, 2)
    attend_turn = after(attend_turn, expand_gradient)
    attend_here = back_end(*attend_turn)
    rows = attend_here.shape[0] // 2
    attend_there = over_x(attend_here[:rows])
    attend_there, output_slopes = after((attend_there, output_slopes))
    output_turn = back_start(output_slopes)
    attend_there = jnp.concatenate([attend_there, over_x(attend_here[rows:])])
    output_here = back_end(*output_turn)
    output_there = over_x(output_here)
    attend_gradient = assemble(attend_here, attend_there, 3)
    output_gradient = assemble(output_here, output_there, 1)

    bias_wide = lax.dynamic_update_slice(
        jnp.zeros((3, PARTS, PART_D), F32), bias_slope.reshape(3, 1, PART_D), (0, part, 0)
    ).reshape(-1)
    small = [bias_wide, attend_gain_part, attend_shift_part, dense_gain_part, dense_shift_part]
    total = small_sum(jnp.concatenate(small))
    index = (lax.axis_index("z") * 2 + y) * 2 + lax.axis_index("c")
    owned, at = [], 0
    for vector, own in zip(small, (attend_bias, attend_gain, attend_shift, dense_gain, dense_shift)):
        size = own.shape[0]
        owned.append(lax.dynamic_slice_in_dim(total, at + index * size, size))
        at += vector.shape[0]
    return (
        layer_output,
        tokens_gradient,
        attend_gradient,
        owned[0],
        output_gradient,
        owned[1],
        owned[2],
        expand_gradient,
        shrink_gradient,
        owned[3],
        owned[4],
    )


def solution(mesh):
    replicas, shard = mesh.shape["replica"], mesh.shape["shard"]
    cut = Mesh(mesh.devices.reshape(replicas, shard // 4, 2, 2), ("x", "z", "y", "c"))
    batch, owner = ("x", "z", "y", "c"), ("z", "y", "c")
    in_specs = (
        P(batch, None),
        P(batch, None),
        P(owner, None),
        P(owner),
        P(owner, None),
        P(owner),
        P(owner),
        P(owner, None),
        P(owner, None),
        P(owner),
        P(owner),
        P(batch, None),
    )
    out_specs = (
        P(batch, None),
        P(batch, None),
        P(owner, None),
        P(owner),
        P(owner, None),
        P(owner),
        P(owner),
        P(owner, None),
        P(owner, None),
        P(owner),
        P(owner),
    )
    return jax.shard_map(shards, mesh=cut, in_specs=in_specs, out_specs=out_specs, check_vma=False)
```
